512 devices in a mesh: box: 128 (over z, y, x_hi), op: 4 (over x_lo, core).
Axes of the slice: x: 4 (x_hi: 2, x_lo: 2; x = x_hi * 2 + x_lo), y: 8, z: 8, core: 2. Of those that a mesh axis runs over, the one named last changes fastest.
Arguments:
- density: float32 [36864, 296], P(('box', 'op')), may hold values from -6 to 6
- operators: float32 [64, 296, 296], P('op'), may hold values from -0.046875 to 0.046875
- owner_count: int32 [128], replicated, may hold values from 96 to 288, as said below
- group_count: int32 [128], replicated, may hold values from 96 to 288, as said below
- target_slot: int32 [128, 64, 288], P('box', 'op'), may hold values from 0 to 288, as said below
- source_box: int32 [128, 64, 288], P('box', 'op'), may hold values from 0 to 24575, as said below
Outputs:
- check_potential: float32 [36864, 296], P(('box', 'op'))
The draws below stay inside these ranges and needn't reach their ends.
Inputs may be any that keep to these rules, and one draw needn't show every extreme that they name: `owner_count`: the counts sum to 24576. The start of owner d and the start of group d (sums of earlier counts) lie within 48 of d * 192, so they differ by at most 96, and some owner holds exactly 288 boxes. `group_count`: the counts sum to 24576, starts as for owner_count; some group holds exactly 288 boxes, and in every draw some group start lies 96 above the owner start of the same index. `target_slot`: entry j of a list of group g holds j or 288; where it holds j, j is below group_count[g]. `source_box`: an entry of group g's lists lies between group_start[g] - 96 and group_start[g + 1] + 96 - 1 (group_start[128] = 24576).
All inputs are finite; a program needn't handle non-finite values.
Results may differ from the reference program's by a relative error of at most 0.0001.
Values sent between devices are 32-bit elements; how exact they have to be, the bound alone decides.
A program may use at most 64 MiB of HBM per device.

```python
import jax
import jax.numpy as jnp
from jax import lax

P_SIZE = 296
BD = 192
OFFSETS = 64
GROUPS = 128
BOXES = 24576
CAP = 288
HALF = 96
SLOTS = 36864


def layout_counts(key):
    base_key = jax.random.fold_in(key, 7)
    key_owner, key_group, key_rank = jax.random.split(base_key, 3)
    quarter = BD // 4
    forced_rank = jax.random.randint(key_rank, (), 2, GROUPS - 2)
    owner_off = jax.random.randint(key_owner, (GROUPS + 1,), -quarter, quarter + 1)
    group_off = jax.random.randint(key_group, (GROUPS + 1,), -quarter, quarter + 1)
    owner_off = owner_off.at[forced_rank].set(-quarter).at[forced_rank + 1].set(quarter).at[forced_rank + 2].set(-quarter)
    group_off = group_off.at[forced_rank - 1].set(-quarter).at[forced_rank].set(quarter).at[forced_rank + 1].set(-quarter)
    owner_off = owner_off.at[0].set(0).at[GROUPS].set(0)
    group_off = group_off.at[0].set(0).at[GROUPS].set(0)
    owner_count = (BD + owner_off[1:] - owner_off[:-1]).astype(jnp.int32)
    group_count = (BD + group_off[1:] - group_off[:-1]).astype(jnp.int32)
    return (owner_count, group_count)


def list_entries(key):
    group_count = layout_counts(key)[1]
    group_start = jnp.cumsum(group_count, dtype=jnp.int32) - group_count
    list_key = jax.random.fold_in(key, 11)
    key_keep, key_move = jax.random.split(list_key, 2)
    shape = (GROUPS, OFFSETS, CAP)
    entry_ids = jnp.arange(CAP, dtype=jnp.int32)[None, None, :]
    offset_ids = jnp.arange(OFFSETS, dtype=jnp.int32)[None, :, None]
    gcount = group_count[:, None, None]
    first_list = offset_ids == 0
    at_start = first_list & (entry_ids == 0)
    at_end = first_list & (entry_ids == gcount - 1)
    keep_entry = jax.random.randint(key_keep, shape, 0, 10) < 7
    keep_entry = keep_entry | at_start | at_end
    live_mask = keep_entry & (entry_ids < gcount)
    target_slot = jnp.where(live_mask, entry_ids, CAP).astype(jnp.int32)
    displace = jax.random.randint(key_move, shape, -HALF, HALF + 1)
    displace = jnp.where(at_start, -HALF, displace)
    displace = jnp.where(at_end, HALF, displace)
    base_box = group_start[:, None, None] + jnp.minimum(entry_ids, gcount - 1)
    source_box = jnp.clip(base_box + displace, 0, BOXES - 1).astype(jnp.int32)
    return (target_slot, source_box)


def draw_owner_count(key, part):
    return layout_counts(key)[0]


def draw_group_count(key, part):
    return layout_counts(key)[1]


def draw_target_slot(key, part):
    return list_entries(key)[0]


def draw_source_box(key, part):
    return list_entries(key)[1]


def steps_of(stream_key, dims, cuts, low, largest):
    loudness = 1.0
    for position, shards_of in cuts:
        heights = jax.random.uniform(jax.random.fold_in(jax.random.fold_in(stream_key, 6), position), (shards_of,), jnp.float32, low / len(cuts), largest / len(cuts))
        loudness = loudness * jnp.repeat(jnp.exp(heights), dims[position] // shards_of).reshape((-1,) + (1,) * (len(dims) - 1 - position))
    return loudness


def noise(own_key, shape, width, most, shards=(), kind=jnp.bfloat16):
    level = steps_of(own_key, shape, shards, -0.22, 0.18) if shards else 1.0
    result = jax.random.normal(own_key, shape, jnp.float32) * width * level
    return jnp.minimum(jnp.maximum(result, -most), most).astype(kind)


def setup_inputs(seed: int = 0) -> dict:
    key_list = jax.random.split(jax.random.key(seed), 7)
    return {
        "density": noise(key_list[0], (SLOTS, P_SIZE), 1.0, 6.0, ((0, 512),), jnp.float32),
        "operators": noise(key_list[1], (OFFSETS, P_SIZE, P_SIZE), (P_SIZE * OFFSETS) ** -0.5, 0.046875, ((0, 4),), jnp.float32),
        "owner_count": draw_owner_count(jax.random.fold_in(key_list[6], 71), 0),
        "group_count": draw_group_count(jax.random.fold_in(key_list[6], 71), 0),
        "target_slot": draw_target_slot(jax.random.fold_in(key_list[6], 71), 0),
        "source_box": draw_source_box(jax.random.fold_in(key_list[6], 71), 0),
    }


def exclusive_starts(counts):
    return jnp.cumsum(counts, dtype=jnp.int32) - counts


def reference(density, operators, owner_count, group_count, target_slot, source_box):
    owner_start = exclusive_starts(owner_count)
    group_start = exclusive_starts(group_count)
    slot_ids = jnp.arange(SLOTS, dtype=jnp.int32)
    owner_ids = slot_ids // CAP
    inner_ids = slot_ids % CAP
    occupied = inner_ids < owner_count[owner_ids]
    morton = jnp.where(occupied, owner_start[owner_ids] + inner_ids, BOXES).astype(jnp.int32)
    box_density = jnp.zeros((BOXES + 1, P_SIZE), jnp.float32).at[morton].set(density)[:BOXES]
    target_box = jnp.where(target_slot < CAP, group_start[:, None, None] + target_slot, BOXES).astype(jnp.int32)

    def offset_step(potential, offset_id):
        source_ids = source_box[:, offset_id, :].reshape(-1)
        target_ids = target_box[:, offset_id, :].reshape(-1)
        source_rows = box_density[source_ids]
        contrib = jnp.dot(source_rows, operators[offset_id].T, precision=lax.Precision.HIGHEST)
        return potential.at[target_ids].add(contrib), None

    potential, _ = lax.scan(offset_step, jnp.zeros((BOXES + 1, P_SIZE), jnp.float32), jnp.arange(OFFSETS, dtype=jnp.int32))
    return jnp.where(occupied[:, None], potential[morton], 0.0)
```

```python
import jax
import jax.numpy as jnp
from jax import lax
from jax.experimental import pallas as pl
from jax.experimental.pallas import tpu as pltpu
from jax.sharding import PartitionSpec as P

MESH = pl.DeviceIdType.MESH
F32, BF16, I32 = jnp.float32, jnp.bfloat16, jnp.int32
ROWS = 72
CAP = 288
EDGE = 96
F = 296
HALF = 152
STEP = 144
OFFS = 16
TILES = 21
SHORT = 15
WIN = 768
KP = 1792


def iota(shape, dim):
    return lax.broadcasted_iota(I32, shape, dim)


def split(v):
    hi = v.astype(BF16)
    lo = (v - hi.astype(F32)).astype(BF16)
    return hi, lo


def slot_of_column(col):
    main = 72 * (col >> 6) + (col & 63)
    c = col & 31
    left = 72 * (c >> 3) + 64 + (c & 7)
    return jnp.where(col < 256, main, left)


def start_at(counts, index):
    lane = iota(counts.shape, 1)
    return jnp.sum(jnp.where(lane < index, counts.astype(F32), 0.0), axis=1, keepdims=True).astype(I32)


def kernel(
    den, ops, ocnt, gcnt, tgt, src, out,
    rx, stage, o_all, x_rows, xt, pmain, pleft, g_all, acc, ufold,
    hot_send, hot_recv, lpack, ra, ral, q_ref, ql_ref, ht, rq, rql, hr, tr, v_ref, fr, fin, tt,
    op_sem, ici_send, sib_send, rsem, osend, orecv,
):
    b, o = lax.axis_index("box"), lax.axis_index("op")
    n = lax.axis_size("box")
    core, chip = o % 2, o // 2
    far, sib = (o + 2) % 4, o + 1 - 2 * core
    up, down = (b + 1) % n, (b + n - 1) % n
    sibling, beside = (b, sib), (b, far)
    peers = [sibling, beside, (up, o), (up, far), (down, o), (down, far)]

    def op_copy(k, slot):
        return pltpu.make_async_copy(ops.at[k], stage.at[slot, pl.ds(0, F)], op_sem.at[slot])

    op_copy(0, 0).start()
    barrier = pltpu.get_barrier_semaphore()
    for peer in peers:
        pl.semaphore_signal(barrier, inc=1, device_id=peer, device_id_type=MESH)

    me = 4 + o
    for lt in range(3):
        parts = [den[8 * (lt + 3 * g) : 8 * (lt + 3 * g) + 8, 256:F] for g in range(3)]
        rx[me, lt] = jnp.concatenate([*parts, jnp.zeros((8, 8), F32)], axis=1)
    for rt in range(9):
        for h in range(2):
            rx[me, 3 + 2 * rt + h] = den[8 * rt : 8 * rt + 8, 128 * h : 128 * h + 128]

    def block_copy(here, there, count, send, device):
        return pltpu.make_async_remote_copy(
            src_ref=rx.at[here, pl.ds(0, count)], dst_ref=rx.at[there, pl.ds(0, count)],
            send_sem=send, recv_sem=rsem.at[there], device_id=device, device_id_type=MESH,
        )

    pl.semaphore_wait(barrier, len(peers))

    def to_prev_segment(i):
        return block_copy(me, o, TILES, ici_send.at[1 + i], peers[2 + i])

    def to_next_segment(i, count):
        return block_copy(me, 8 + o, count, ici_send.at[3 + i], peers[4 + i])

    to_beside = block_copy(me, me, TILES, ici_send.at[0], beside)
    to_sibling = block_copy(me, me, TILES, sib_send.at[0], sibling)
    for i in (1, 0):
        to_prev_segment(i).start()

        @pl.when(o < 2)
        def _():
            to_next_segment(i, TILES).start()

        @pl.when(o == 2)
        def _():
            to_next_segment(i, SHORT).start()

    to_beside.start()
    to_sibling.start()

    counts_o, counts_g = ocnt[...], gcnt[...]
    os0, os1, os2 = (start_at(counts_o, b + i) for i in (-1, 0, 1))
    gs1, gs2 = (start_at(counts_g, b + i) for i in (0, 1))
    shift = gs1 - os1
    m = src[0]
    place = jnp.where(m < os1, m - os0, jnp.where(m < os2, CAP + m - os1, 2 * CAP + m - os2))
    place = jnp.where(tgt[0] < CAP, place, -1)
    j = iota((CAP, 384), 0) + shift
    j = jnp.where(j < 0, j + CAP, jnp.where(j >= CAP, j - CAP, j))
    turn = jnp.where(j == slot_of_column(iota((CAP, 384), 1)), 1.0, 0.0).astype(F32)
    turned = jnp.dot(place.astype(F32), turn, precision=lax.Precision.HIGHEST, preferred_element_type=F32)
    turned = (turned + 0.25 * jnp.where(turned < 0, -1.0, 1.0)).astype(I32)
    pmain[...] = turned[:, :256]
    group_of_lane = iota((1, 128), 1) >> 5
    for t in range(2):
        rows = []
        for h in range(2):
            row = jnp.zeros((1, 128), I32)
            for a in range(4):
                k = 8 * t + 4 * h + a
                row = jnp.where(group_of_lane == a, turned[k : k + 1, 256:384], row)
            rows.append(row)
        pleft[t : t + 1] = jnp.concatenate(rows, axis=1)

    s = slot_of_column(iota((384, 128), 0))
    real = iota((384, 128), 0) < CAP
    lane = iota((384, 128), 1)
    is_head = real & (s >= CAP - EDGE) & (os1 + s - CAP >= gs1) & (s - (CAP - EDGE) == lane)
    box1 = os1 + s
    tail = jnp.where((box1 >= os2) & (box1 < gs2), box1 - os2, jnp.where(box1 + CAP < gs2, box1 + CAP - os2, -1))
    hot_send[:, :128] = jnp.where(is_head, 1.0, 0.0).astype(BF16)
    hot_send[:, 128:] = jnp.where(real & (tail == lane), 1.0, 0.0).astype(BF16)
    r = iota((256, 128), 0)
    slot = jnp.where(r < 128, os2 - os1 + r - EDGE, r - 128)
    known = jnp.where(r < 128, r, r - 128) < EDGE
    lane = iota((256, 128), 1)
    hot_recv[:, :128] = jnp.where(known & (slot == slot_of_column(lane + 128 * chip)), 1.0, 0.0).astype(BF16)
    hot_recv[:, 128:] = jnp.where(known & (lane < 32) & (slot == slot_of_column(lane + 256)), 1.0, 0.0).astype(BF16)

    stage[:, pl.ds(F, 8), :] = jnp.zeros((2, 8, F), F32)

    def split_pair(q, _):
        for par in range(2):
            k = 2 * q + par

            @pl.when(k < OFFS - 1)
            def _():
                op_copy(k + 1, 1 - par).start()

            op_copy(k, par).wait()
            v = stage[par]
            hi = v.astype(BF16)
            hi32 = hi.astype(F32)
            lo32 = v - hi32
            base = 768 * par
            o_all[q, :, base : base + 256] = hi[:, :256]
            o_all[q, :, base + 256 : base + 512] = hi[:, :256]
            o_all[q, :, base + 512 : base + 768] = lo32[:, :256].astype(BF16)
            last = jnp.concatenate([hi32[:, 256:], hi32[:, 256:], lo32[:, 256:], jnp.zeros((304, 8), F32)], axis=1)
            o_all[q, :, 1536 + 128 * par : 1664 + 128 * par] = last.astype(BF16)
        return 0

    lax.fori_loop(0, OFFS // 2, split_pair, 0)

    def arrived(there, count=TILES):
        block_copy(there, there, count, ici_send.at[0], sibling).wait_recv()

    def hand_on(i, there, count=TILES):
        return block_copy(there, there, count, sib_send.at[i], sibling)

    passed = [4 + far, o, far, 8 + core]
    for i, there in enumerate(passed):
        arrived(there)
        hand_on(1 + i, there).start()

    @pl.when(core == 0)
    def _():
        arrived(10, SHORT)
        hand_on(5, 10, SHORT).start()

    for there in (4 + sib, 4 + (sib + 2) % 4, sib, (sib + 2) % 4, 8 + 1 - core):
        arrived(there)

    @pl.when(core == 1)
    def _():
        arrived(10, SHORT)

    def unpack(idx, rts):
        base = pl.multiple_of(ROWS * idx, 8)
        for rt in rts:
            at = pl.ds(base + 8 * rt, 8)
            for h in range(2):
                x_rows[at, 128 * h : 128 * h + 128] = rx[idx, 3 + 2 * rt + h]
            g = rt // 3
            left = rx[idx, rt % 3]
            x_rows[at, 256:384] = pltpu.roll(left, 128 - 40 * g, 1) if g else left

    def unpack_full(idx, _):
        unpack(idx, range(9))
        return 0

    lax.fori_loop(0, 10, unpack_full, 0)
    unpack(10, range(6))

    for i in range(WIN // 128):
        t = x_rows[128 * i : 128 * i + 128, :].T
        hi32 = t.astype(BF16).astype(F32)
        lo32 = t - hi32
        xt[:, 128 * i : 128 * i + 128] = jnp.concatenate(
            [hi32[:256], lo32[:256], hi32[256:F], lo32[256:F]], axis=0
        ).astype(BF16)

    def gathered(row):
        hot = jnp.where(iota((WIN, 256), 0) == row, 1.0, 0.0).astype(BF16)
        return jnp.dot(xt[...], hot, preferred_element_type=F32)

    def last_rows(g):
        return jnp.concatenate([g[512:592], g[512:552], jnp.zeros((8, g.shape[1]), F32)], axis=0).astype(BF16)

    def gather_pair(q, _):
        for par in range(2):
            g = gathered(pmain[pl.ds(2 * q + par, 1), :])
            hi, lo = g[:256].astype(BF16), g[256:512].astype(BF16)
            base = 768 * par
            g_all[q, base : base + 256, :256] = hi
            g_all[q, base + 256 : base + 512, :256] = lo
            g_all[q, base + 512 : base + 768, :256] = hi
            g_all[q, 1536 + 128 * par : 1664 + 128 * par, :256] = last_rows(g)
        return 0

    lax.fori_loop(0, OFFS // 2, gather_pair, 0)

    def gather_left(t, _):
        g = gathered(pleft[pl.ds(t, 1), :])
        for kk in range(8):
            h, a = kk // 4, kk % 4
            part = jnp.where(group_of_lane == a, g[:, 128 * h : 128 * h + 128], 0.0)
            hi, lo = part[:256].astype(BF16), part[256:512].astype(BF16)
            q, base = 4 * t + kk // 2, 768 * (kk % 2)
            g_all[q, base : base + 256, 256:] = hi
            g_all[q, base + 256 : base + 512, 256:] = lo
            g_all[q, base + 512 : base + 768, 256:] = hi
            g_all[q, 1536 + 128 * (kk % 2) : 1664 + 128 * (kk % 2), 256:] = last_rows(part)
        return 0

    lax.fori_loop(0, 2, gather_left, 0)

    acc[...] = jnp.dot(o_all[0], g_all[0], preferred_element_type=F32)

    def multiply(q, _):
        acc[...] += jnp.dot(o_all[q], g_all[q], preferred_element_type=F32)
        return 0

    lax.fori_loop(1, OFFS // 2, multiply, 0)

    u = acc[:, 256:384]
    u = u + pltpu.roll(u, 64, 1)
    ufold[...] = u + pltpu.roll(u, 32, 1)

    def packed(half):
        v = ufold[pl.ds(pl.multiple_of(STEP * half, 8), 160), :]
        row = jnp.zeros((40, 128), F32)
        for a in range(4):
            row = jnp.where(group_of_lane == a, v[40 * a : 40 * a + 40], row)
        return row

    def unpacked(v):
        parts = [v if a == 0 else pltpu.roll(v, 128 - 32 * a, 1) for a in range(4)]
        return jnp.concatenate(parts, axis=0)[:HALF]

    def send(i, source, target, device, recv=None):
        return pltpu.make_async_remote_copy(
            src_ref=source, dst_ref=target, send_sem=osend.at[i], recv_sem=orecv.at[i if recv is None else recv],
            device_id=device, device_id_type=MESH,
        )

    theirs = pl.ds(pl.multiple_of(STEP * (1 - core), 8), HALF)
    mine = pl.ds(pl.multiple_of(STEP * core, 8), HALF)
    lpack[...] = packed(1 - core)
    swap = [send(0, acc.at[theirs, pl.ds(0, 256)], ra, sibling), send(1, lpack, ral, sibling)]
    for c in swap:
        c.start()
    own_left = packed(core)
    for c in swap:
        c.wait_recv()
    q0 = acc[mine, :128] + ra[:, :128]
    q1 = acc[mine, 128:256] + ra[:, 128:]
    ql = own_left + ral[...]
    q_ref[0], q_ref[1], ql_ref[...] = q0, q1, ql

    cross = [send(2, q_ref.at[1 - chip], rq, beside), send(3, ql_ref, rql, beside)]
    for c in cross:
        c.start()
    hi, lo = split(jnp.concatenate([q0, q1, unpacked(ql)], axis=1))
    edges = jnp.dot(hi, hot_send[...], preferred_element_type=F32) + jnp.dot(
        lo, hot_send[...], preferred_element_type=F32
    )
    ht[0], ht[1] = edges[:, :128], edges[:, 128:]
    heads = [send(4 + i, ht.at[0], hr.at[chip], peers[4 + i], 4 + chip) for i in range(2)]
    tails = send(6, ht.at[1], tr.at[chip], (up, core), 6 + chip)
    for c in (heads[1], tails, heads[0]):
        c.start()
    for c in cross:
        c.wait_recv()
    s = slot_of_column(iota((1, 128), 1) + 128 * chip)
    box1 = os1 + s
    keep = (box1 >= gs1) & (box1 < gs2) & (box1 < os2)
    own = jnp.where(keep, q_ref[chip] + rq[...], 0.0)
    box1 = os1 + slot_of_column(256 + (iota((1, 128), 1) & 31))
    keep = (box1 >= gs1) & (box1 < gs2) & (box1 < os2)
    own_left = unpacked(jnp.where(keep, ql_ref[...] + rql[...], 0.0))
    for i in range(2):
        send(4 + i, ht.at[0], hr.at[i], peers[4], 4 + i).wait_recv()

    @pl.when(chip == 0)
    def _():
        for i in range(2):
            send(6, ht.at[1], tr.at[i], peers[4], 6 + i).wait_recv()

    @pl.when(chip == 1)
    def _():
        tr[...] = jnp.zeros(tr.shape, F32)

    hi, lo = split(jnp.concatenate([hr[0] + hr[1], tr[0] + tr[1]], axis=1))
    moved = jnp.dot(hi, hot_recv[...], preferred_element_type=F32) + jnp.dot(
        lo, hot_recv[...], preferred_element_type=F32
    )
    v0, v1 = own + moved[:, :128], own_left + moved[:, 128:]
    v_ref[0], v_ref[1] = v0, v1
    last = send(8, v_ref, fr, sibling)
    last.start()
    for i, v in enumerate((v0, v1)):
        fin[i, mine] = v
    last.wait_recv()
    for i in range(2):
        fin[i, theirs] = fr[i]
        tt[i] = fin[i].T
    out[0:64] = tt[0, pl.ds(pl.multiple_of(64 * core, 8), 64), :F]
    out[64:72] = tt[1, pl.ds(pl.multiple_of(8 * o, 8), 8), :F]

    for c in (to_beside, to_sibling, *(to_prev_segment(i) for i in range(2))):
        c.wait_send()
    for i, there in enumerate(passed):
        hand_on(1 + i, there).wait_send()

    @pl.when(core == 0)
    def _():
        hand_on(5, 10, SHORT).wait_send()

    @pl.when(o < 2)
    def _():
        for i in range(2):
            to_next_segment(i, TILES).wait_send()

    @pl.when(o == 2)
    def _():
        for i in range(2):
            to_next_segment(i, SHORT).wait_send()

    for c in (*swap, *cross, *heads, tails, last):
        c.wait_send()


def body(density, operators, owner_count, group_count, target_slot, source_box):
    vmem = pl.BlockSpec(memory_space=pltpu.VMEM)
    scratch = [
        pltpu.VMEM((12, TILES, 8, 128), F32),
        pltpu.VMEM((2, 304, F), F32),
        pltpu.VMEM((OFFS // 2, 304, KP), BF16),
        pltpu.VMEM((WIN, 384), F32),
        pltpu.VMEM((592, WIN), BF16),
        pltpu.VMEM((OFFS, 256), I32),
        pltpu.VMEM((2, 256), I32),
        pltpu.VMEM((OFFS // 2, KP, 384), BF16),
        pltpu.VMEM((304, 384), F32),
        pltpu.VMEM((304, 128), F32),
        pltpu.VMEM((384, 256), BF16),
        pltpu.VMEM((256, 256), BF16),
        pltpu.VMEM((40, 128), F32),
        pltpu.VMEM((HALF, 256), F32),
        pltpu.VMEM((40, 128), F32),
        pltpu.VMEM((2, HALF, 128), F32),
        pltpu.VMEM((40, 128), F32),
        pltpu.VMEM((2, HALF, 128), F32),
        pltpu.VMEM((HALF, 128), F32),
        pltpu.VMEM((40, 128), F32),
        pltpu.VMEM((2, HALF, 128), F32),
        pltpu.VMEM((2, HALF, 128), F32),
        pltpu.VMEM((2, HALF, 128), F32),
        pltpu.VMEM((2, HALF, 128), F32),
        pltpu.VMEM((2, 384, 128), F32),
        pltpu.VMEM((2, 128, 384), F32),
        pltpu.SemaphoreType.DMA((2,)),
        pltpu.SemaphoreType.DMA((5,)),
        pltpu.SemaphoreType.DMA((6,)),
        pltpu.SemaphoreType.DMA((12,)),
        pltpu.SemaphoreType.DMA((9,)),
        pltpu.SemaphoreType.DMA((9,)),
    ]
    return pl.pallas_call(
        kernel,
        out_shape=jax.ShapeDtypeStruct((ROWS, F), F32),
        in_specs=[vmem, pl.BlockSpec(memory_space=pl.ANY), vmem, vmem, vmem, vmem],
        out_specs=vmem,
        scratch_shapes=scratch,
        compiler_params=pltpu.CompilerParams(
            collective_id=0, has_side_effects=True, vmem_limit_bytes=48 * 2**20
        ),
        name="translate",
    )(density, operators, owner_count[None], group_count[None], target_slot, source_box)


def solution(mesh):
    placed = (P(("box", "op"), None), P("op", None, None), P(), P(), P("box", "op", None), P("box", "op", None))
    return jax.shard_map(
        body, mesh=mesh, in_specs=placed, out_specs=P(("box", "op"), None), check_vma=False
    )
```

```python
import jax
import jax.numpy as jnp
from jax import lax
from jax.experimental import pallas as pl
from jax.experimental.pallas import tpu as pltpu
from jax.sharding import PartitionSpec as P

MESH = pl.DeviceIdType.MESH
F32, BF16, I32 = jnp.float32, jnp.bfloat16, jnp.int32
ROWS = 72
CAP = 288
EDGE = 96
F = 296
HALF = 152
STEP = 144
OFFS = 16
TILES = 21
SHORT = 15
WIN = 768


def iota(shape, dim):
    return lax.broadcasted_iota(I32, shape, dim)


def split(v):
    hi = v.astype(BF16)
    lo = (v - hi.astype(F32)).astype(BF16)
    return hi, lo


def slot_of_column(col):
    main = 72 * (col >> 6) + (col & 63)
    c = col & 31
    left = 72 * (c >> 3) + 64 + (c & 7)
    return jnp.where(col < 256, main, left)


def start_at(counts, index):
    lane = iota(counts.shape, 1)
    return jnp.sum(jnp.where(lane < index, counts.astype(F32), 0.0), axis=1, keepdims=True).astype(I32)


def kernel(
    den_hbm, ops, ocnt_hbm, gcnt_hbm, tgt_hbm, src_hbm, out,
    den, ocnt, gcnt, tgt, src, rx, stage, o_main, o_left, xt, pmain, pleft, g_hi, g_lo, g_last, acc, ufold,
    hot_send, hot_recv, lpack, ra, ral, q_ref, ql_ref, ht, rq, rql, hr, tr, v_ref, fr, fin, tt,
    in_sem, op_sem, ici_send, sib_send, rsem, osend, orecv,
):
    b, o = lax.axis_index("box"), lax.axis_index("op")
    n = lax.axis_size("box")
    core, chip = o % 2, o // 2
    far, sib = (o + 2) % 4, o + 1 - 2 * core
    up, down = (b + 1) % n, (b + n - 1) % n
    sibling, beside = (b, sib), (b, far)
    peers = [sibling, beside, (up, o), (up, far), (down, o), (down, far)]

    def op_copy(k):
        return pltpu.make_async_copy(ops.at[k], stage.at[k, pl.ds(0, F)], op_sem.at[k])

    barrier = pltpu.get_barrier_semaphore()
    for peer in peers:
        pl.semaphore_signal(barrier, inc=1, device_id=peer, device_id_type=MESH)
    pairs = ((den_hbm, den), (ocnt_hbm, ocnt), (gcnt_hbm, gcnt), (tgt_hbm, tgt), (src_hbm, src))
    inputs = [pltpu.make_async_copy(a, v, in_sem.at[i]) for i, (a, v) in enumerate(pairs)]
    for c in inputs:
        c.start()
    for k in range(OFFS):
        op_copy(k).start()
    inputs[0].wait()

    me = 4 + o
    for lt in range(3):
        parts = [den[8 * (lt + 3 * g) : 8 * (lt + 3 * g) + 8, 256:F] for g in range(3)]
        rx[me, lt] = jnp.concatenate([*parts, jnp.zeros((8, 8), F32)], axis=1)
    for rt in range(9):
        for h in range(2):
            rx[me, 3 + 2 * rt + h] = den[8 * rt : 8 * rt + 8, 128 * h : 128 * h + 128]

    def block_copy(here, there, count, send, device):
        return pltpu.make_async_remote_copy(
            src_ref=rx.at[here, pl.ds(0, count)], dst_ref=rx.at[there, pl.ds(0, count)],
            send_sem=send, recv_sem=rsem.at[there], device_id=device, device_id_type=MESH,
        )

    pl.semaphore_wait(barrier, len(peers))

    def to_prev_segment(i):
        return block_copy(me, o, TILES, ici_send.at[1 + i], peers[2 + i])

    def to_next_segment(i, count):
        return block_copy(me, 8 + o, count, ici_send.at[3 + i], peers[4 + i])

    to_beside = block_copy(me, me, TILES, ici_send.at[0], beside)
    to_sibling = block_copy(me, me, TILES, sib_send.at[0], sibling)
    for i in (1, 0):
        to_prev_segment(i).start()

        @pl.when(o < 2)
        def _():
            to_next_segment(i, TILES).start()

        @pl.when(o == 2)
        def _():
            to_next_segment(i, SHORT).start()

    to_beside.start()
    to_sibling.start()

    for c in inputs[1:]:
        c.wait()
    counts_o, counts_g = ocnt[...], gcnt[...]
    os0, os1, os2 = (start_at(counts_o, b + i) for i in (-1, 0, 1))
    gs1, gs2 = (start_at(counts_g, b + i) for i in (0, 1))
    shift = gs1 - os1
    m = src[0]
    place = jnp.where(m < os1, m - os0 + 480, jnp.where(m < os2, m - os1, m - os2 + CAP))
    place = jnp.where(tgt[0] < CAP, place, -1)
    j = iota((CAP, 384), 0) + shift
    j = jnp.where(j < 0, j + CAP, jnp.where(j >= CAP, j - CAP, j))
    turn = jnp.where(j == slot_of_column(iota((CAP, 384), 1)), 1.0, 0.0).astype(F32)
    turned = jnp.dot(place.astype(F32), turn, precision=lax.Precision.HIGHEST, preferred_element_type=F32)
    turned = (turned + 0.25 * jnp.where(turned < 0, -1.0, 1.0)).astype(I32)
    pmain[...] = turned[:, :256]
    group_of_lane = iota((1, 128), 1) >> 5
    for t in range(2):
        rows = []
        for h in range(2):
            row = jnp.zeros((1, 128), I32)
            for a in range(4):
                k = 8 * t + 4 * h + a
                row = jnp.where(group_of_lane == a, turned[k : k + 1, 256:384], row)
            rows.append(row)
        pleft[t : t + 1] = jnp.concatenate(rows, axis=1)

    s = slot_of_column(iota((384, 128), 0))
    real = iota((384, 128), 0) < CAP
    lane = iota((384, 128), 1)
    is_head = real & (s >= CAP - EDGE) & (os1 + s - CAP >= gs1) & (s - (CAP - EDGE) == lane)
    box1 = os1 + s
    tail = jnp.where((box1 >= os2) & (box1 < gs2), box1 - os2, jnp.where(box1 + CAP < gs2, box1 + CAP - os2, -1))
    hot_send[:, :128] = jnp.where(is_head, 1.0, 0.0).astype(BF16)
    hot_send[:, 128:] = jnp.where(real & (tail == lane), 1.0, 0.0).astype(BF16)
    r = iota((256, 128), 0)
    slot = jnp.where(r < 128, os2 - os1 + r - EDGE, r - 128)
    known = jnp.where(r < 128, r, r - 128) < EDGE
    lane = iota((256, 128), 1)
    hot_recv[:, :128] = jnp.where(known & (slot == slot_of_column(lane + 128 * chip)), 1.0, 0.0).astype(BF16)
    hot_recv[:, 128:] = jnp.where(known & (lane < 32) & (slot == slot_of_column(lane + 256)), 1.0, 0.0).astype(BF16)

    stage[:, pl.ds(F, 8), :] = jnp.zeros((OFFS, 8, F), F32)

    def split_pair(q, _):
        for par in range(2):
            k = 2 * q + par
            op_copy(k).wait()
            v = stage[k]
            hi = v.astype(BF16)
            hi32 = hi.astype(F32)
            lo32 = v - hi32
            o_main[q, :304, 256 * par : 256 * par + 256] = hi[:, :256]
            o_main[q, 304:, 256 * par : 256 * par + 256] = lo32[:, :256].astype(BF16)
            last = jnp.concatenate([hi32[:, 256:], hi32[:, 256:], lo32[:, 256:], jnp.zeros((304, 8), F32)], axis=1)
            o_left[q, :, 128 * par : 128 * par + 128] = last.astype(BF16)
        return 0

    def arrived(there, count=TILES):
        block_copy(there, there, count, ici_send.at[0], sibling).wait_recv()

    def hand_on(i, there, count=TILES):
        return block_copy(there, there, count, sib_send.at[i], sibling)

    def pass_own():
        arrived(4 + far)
        hand_on(1, 4 + far).start()

    def pass_prev():
        for i, there in ((2, o), (3, far)):
            arrived(there)
            hand_on(i, there).start()

    def pass_next():
        arrived(8 + core)
        hand_on(4, 8 + core).start()

        @pl.when(core == 0)
        def _():
            arrived(10, SHORT)
            hand_on(5, 10, SHORT).start()

    order = [(idx, rt) for idx in (4, 5, 6, 7, 8, 9, 10, 0, 1, 2, 3) for rt in range(6 if idx == 10 else 9)]

    def turn_rows(i):
        tiles = order[16 * i : 16 * i + 16]
        wide = [jnp.concatenate([rx[idx, 3 + 2 * rt + h] for idx, rt in tiles], axis=0).T for h in range(2)]
        left = [
            pltpu.roll(rx[idx, rt % 3], 128 - 40 * (rt // 3), 1) if rt >= 3 else rx[idx, rt % 3] for idx, rt in tiles
        ]
        t = jnp.concatenate([*wide, jnp.concatenate(left, axis=0).T[:40]], axis=0)
        hi32 = t.astype(BF16).astype(F32)
        lo32 = t - hi32
        xt[:, 128 * i : 128 * i + 128] = jnp.concatenate(
            [hi32[:256], lo32[:256], hi32[256:F], lo32[256:F]], axis=0
        ).astype(BF16)

    def gathered(row, first, last):
        hot = jnp.where(iota((last - first, 256), 0) + first == row, 1.0, 0.0).astype(BF16)
        return jnp.dot(xt[:, first:last], hot, preferred_element_type=F32)

    def put(q, par, columns, g, add):
        tail = jnp.concatenate([g[512:592], g[512:552], jnp.zeros((8, g.shape[1]), F32)], axis=0)
        for ref, at, v in (
            (g_hi, pl.ds(256 * par, 256), g[:256]),
            (g_lo, pl.ds(256 * par, 256), g[256:512]),
            (g_last, pl.ds(128 * par, 128), tail),
        ):
            v = v.astype(BF16)
            ref[q, at, columns] = ref[q, at, columns] + v if add else v

    def gather(first, last):
        add = first > 0

        def gather_pair(q, _):
            for par in range(2):
                put(q, par, pl.ds(0, 256), gathered(pmain[pl.ds(2 * q + par, 1), :], first, last), add)
            return 0

        lax.fori_loop(0, OFFS // 2, gather_pair, 0)

        def gather_left(t, _):
            g = gathered(pleft[pl.ds(t, 1), :], first, last)
            for kk in range(8):
                h, a = kk // 4, kk % 4
                part = jnp.where(group_of_lane == a, g[:, 128 * h : 128 * h + 128], 0.0)
                put(4 * t + kk // 2, kk % 2, pl.ds(256, 128), part, add)
            return 0

        lax.fori_loop(0, 2, gather_left, 0)

    lax.fori_loop(0, OFFS // 4, split_pair, 0)
    pass_own()
    lax.fori_loop(OFFS // 4, OFFS // 2, split_pair, 0)
    even = b % 2 == 0
    pl.when(even)(pass_next)
    pl.when(jnp.logical_not(even))(pass_prev)
    arrived(4 + sib)
    arrived(4 + (sib + 2) % 4)
    turn_rows(0)
    turn_rows(1)
    gather(0, 256)
    pl.when(even)(pass_prev)
    pl.when(jnp.logical_not(even))(pass_next)
    for there in (sib, (sib + 2) % 4, 9 - core):
        arrived(there)

    @pl.when(core == 1)
    def _():
        arrived(10, SHORT)

    for i in range(2, WIN // 128):
        turn_rows(i)
    gather(256, WIN)

    def product(q):
        both = jnp.dot(o_main[q], g_hi[q], preferred_element_type=F32)
        third = jnp.dot(o_main[q, :304], g_lo[q], preferred_element_type=F32)
        return both[:304] + both[304:] + third + jnp.dot(o_left[q], g_last[q], preferred_element_type=F32)

    acc[...] = product(0)

    def multiply(q, _):
        acc[...] += product(q)
        return 0

    lax.fori_loop(1, OFFS // 2, multiply, 0)

    u = acc[:, 256:384]
    u = u + pltpu.roll(u, 64, 1)
    ufold[...] = u + pltpu.roll(u, 32, 1)

    def packed(half):
        v = ufold[pl.ds(pl.multiple_of(STEP * half, 8), 160), :]
        row = jnp.zeros((40, 128), F32)
        for a in range(4):
            row = jnp.where(group_of_lane == a, v[40 * a : 40 * a + 40], row)
        return row

    def unpacked(v):
        parts = [v if a == 0 else pltpu.roll(v, 128 - 32 * a, 1) for a in range(4)]
        return jnp.concatenate(parts, axis=0)[:HALF]

    def send(i, source, target, device, recv=None):
        return pltpu.make_async_remote_copy(
            src_ref=source, dst_ref=target, send_sem=osend.at[i], recv_sem=orecv.at[i if recv is None else recv],
            device_id=device, device_id_type=MESH,
        )

    theirs = pl.ds(pl.multiple_of(STEP * (1 - core), 8), HALF)
    mine = pl.ds(pl.multiple_of(STEP * core, 8), HALF)
    lpack[...] = packed(1 - core)
    swap = [send(0, acc.at[theirs, pl.ds(0, 256)], ra, sibling), send(1, lpack, ral, sibling)]
    for c in swap:
        c.start()
    own_left = packed(core)
    for c in swap:
        c.wait_recv()
    q0 = acc[mine, :128] + ra[:, :128]
    q1 = acc[mine, 128:256] + ra[:, 128:]
    ql = own_left + ral[...]
    q_ref[0], q_ref[1], ql_ref[...] = q0, q1, ql

    cross = [send(2, q_ref.at[1 - chip], rq, beside), send(3, ql_ref, rql, beside)]
    for c in cross:
        c.start()
    hi, lo = split(jnp.concatenate([q0, q1, unpacked(ql)], axis=1))
    edges = jnp.dot(hi, hot_send[...], preferred_element_type=F32) + jnp.dot(
        lo, hot_send[...], preferred_element_type=F32
    )
    ht[0], ht[1] = edges[:, :128], edges[:, 128:]
    heads = [send(4 + i, ht.at[0], hr.at[chip], peers[4 + i], 4 + chip) for i in range(2)]
    tails = send(6, ht.at[1], tr.at[chip], (up, core), 6 + chip)
    for c in (heads[1], tails, heads[0]):
        c.start()
    for c in cross:
        c.wait_recv()
    s = slot_of_column(iota((1, 128), 1) + 128 * chip)
    box1 = os1 + s
    keep = (box1 >= gs1) & (box1 < gs2) & (box1 < os2)
    own = jnp.where(keep, q_ref[chip] + rq[...], 0.0)
    box1 = os1 + slot_of_column(256 + (iota((1, 128), 1) & 31))
    keep = (box1 >= gs1) & (box1 < gs2) & (box1 < os2)
    own_left = unpacked(jnp.where(keep, ql_ref[...] + rql[...], 0.0))
    for i in range(2):
        send(4 + i, ht.at[0], hr.at[i], peers[4], 4 + i).wait_recv()

    @pl.when(chip == 0)
    def _():
        for i in range(2):
            send(6, ht.at[1], tr.at[i], peers[4], 6 + i).wait_recv()

    @pl.when(chip == 1)
    def _():
        tr[...] = jnp.zeros(tr.shape, F32)

    hi, lo = split(jnp.concatenate([hr[0] + hr[1], tr[0] + tr[1]], axis=1))
    moved = jnp.dot(hi, hot_recv[...], preferred_element_type=F32) + jnp.dot(
        lo, hot_recv[...], preferred_element_type=F32
    )
    v0, v1 = own + moved[:, :128], own_left + moved[:, 128:]
    v_ref[0], v_ref[1] = v0, v1
    last = send(8, v_ref, fr, sibling)
    last.start()
    for i, v in enumerate((v0, v1)):
        fin[i, mine] = v
    last.wait_recv()
    for i in range(2):
        fin[i, theirs] = fr[i]
        tt[i] = fin[i].T
    out[0:64] = tt[0, pl.ds(pl.multiple_of(64 * core, 8), 64), :F]
    out[64:72] = tt[1, pl.ds(pl.multiple_of(8 * o, 8), 8), :F]

    for c in (to_beside, to_sibling, *(to_prev_segment(i) for i in range(2))):
        c.wait_send()
    for i, there in enumerate((4 + far, o, far, 8 + core)):
        hand_on(1 + i, there).wait_send()

    @pl.when(core == 0)
    def _():
        hand_on(5, 10, SHORT).wait_send()

    @pl.when(o < 2)
    def _():
        for i in range(2):
            to_next_segment(i, TILES).wait_send()

    @pl.when(o == 2)
    def _():
        for i in range(2):
            to_next_segment(i, SHORT).wait_send()

    for c in (*swap, *cross, *heads, tails, last):
        c.wait_send()


def body(density, operators, owner_count, group_count, target_slot, source_box):
    vmem = pl.BlockSpec(memory_space=pltpu.VMEM)
    scratch = [
        pltpu.VMEM((ROWS, F), F32),
        pltpu.VMEM(owner_count[None].shape, I32),
        pltpu.VMEM(group_count[None].shape, I32),
        pltpu.VMEM((1, OFFS, CAP), I32),
        pltpu.VMEM((1, OFFS, CAP), I32),
        pltpu.VMEM((12, TILES, 8, 128), F32),
        pltpu.VMEM((OFFS, 304, F), F32),
        pltpu.VMEM((OFFS // 2, 608, 512), BF16),
        pltpu.VMEM((OFFS // 2, 304, 256), BF16),
        pltpu.VMEM((592, WIN), BF16),
        pltpu.VMEM((OFFS, 256), I32),
        pltpu.VMEM((2, 256), I32),
        pltpu.VMEM((OFFS // 2, 512, 384), BF16),
        pltpu.VMEM((OFFS // 2, 512, 384), BF16),
        pltpu.VMEM((OFFS // 2, 256, 384), BF16),
        pltpu.VMEM((304, 384), F32),
        pltpu.VMEM((304, 128), F32),
        pltpu.VMEM((384, 256), BF16),
        pltpu.VMEM((256, 256), BF16),
        pltpu.VMEM((40, 128), F32),
        pltpu.VMEM((HALF, 256), F32),
        pltpu.VMEM((40, 128), F32),
        pltpu.VMEM((2, HALF, 128), F32),
        pltpu.VMEM((40, 128), F32),
        pltpu.VMEM((2, HALF, 128), F32),
        pltpu.VMEM((HALF, 128), F32),
        pltpu.VMEM((40, 128), F32),
        pltpu.VMEM((2, HALF, 128), F32),
        pltpu.VMEM((2, HALF, 128), F32),
        pltpu.VMEM((2, HALF, 128), F32),
        pltpu.VMEM((2, HALF, 128), F32),
        pltpu.VMEM((2, 384, 128), F32),
        pltpu.VMEM((2, 128, 384), F32),
        pltpu.SemaphoreType.DMA((5,)),
        pltpu.SemaphoreType.DMA((OFFS,)),
        pltpu.SemaphoreType.DMA((5,)),
        pltpu.SemaphoreType.DMA((6,)),
        pltpu.SemaphoreType.DMA((12,)),
        pltpu.SemaphoreType.DMA((9,)),
        pltpu.SemaphoreType.DMA((9,)),
    ]
    return pl.pallas_call(
        kernel,
        out_shape=jax.ShapeDtypeStruct((ROWS, F), F32),
        in_specs=[pl.BlockSpec(memory_space=pltpu.HBM)] * 6,
        out_specs=vmem,
        scratch_shapes=scratch,
        compiler_params=pltpu.CompilerParams(
            collective_id=0, has_side_effects=True, vmem_limit_bytes=60 * 2**20
        ),
        name="translate",
    )(density, operators, owner_count[None], group_count[None], target_slot, source_box)


def solution(mesh):
    placed = (P(("box", "op"), None), P("op", None, None), P(), P(), P("box", "op", None), P("box", "op", None))
    return jax.shard_map(
        body, mesh=mesh, in_specs=placed, out_specs=P(("box", "op"), None), check_vma=False
    )
```

```python
import jax
import jax.numpy as jnp
from jax import lax
from jax.experimental import pallas as pl
from jax.experimental.pallas import tpu as pltpu
from jax.sharding import PartitionSpec as P

MESH = pl.DeviceIdType.MESH
F32, BF16, I32 = jnp.float32, jnp.bfloat16, jnp.int32
ROWS = 72
CAP = 288
EDGE = 96
F = 296
HALF = 152
STEP = 144
OFFS = 16
TILES = 21
SHORT = 15


def iota(shape, dim):
    return lax.broadcasted_iota(I32, shape, dim)


def split(v):
    hi = v.astype(BF16)
    lo = (v - hi.astype(F32)).astype(BF16)
    return hi, lo


def slot_of_column(col):
    main = 72 * (col >> 6) + (col & 63)
    c = col & 31
    left = 72 * (c >> 3) + 64 + (c & 7)
    return jnp.where(col < 256, main, left)


def start_at(counts, index):
    lane = iota(counts.shape, 1)
    return jnp.sum(jnp.where(lane < index, counts.astype(F32), 0.0), axis=1, keepdims=True).astype(I32)


def kernel(
    den_hbm, ops, ocnt_hbm, gcnt_hbm, tgt_hbm, src_hbm, out,
    den, ocnt, gcnt, tgt, src, rx, stage, o_main, o_left, xt, pmain, pleft, g_hi, g_lo, g_last, acc, ufold,
    hot_send, hot_recv, lpack, ra, ral, q_ref, ql_ref, ht, rq, rql, hr, tr, v_ref, fr, fin, tt,
    in_sem, op_sem, ici_send, sib_send, rsem, osend, orecv,
):
    b, o = lax.axis_index("box"), lax.axis_index("op")
    n = lax.axis_size("box")
    core, chip = o % 2, o // 2
    far, sib = (o + 2) % 4, o + 1 - 2 * core
    up, down = (b + 1) % n, (b + n - 1) % n
    sibling, beside = (b, sib), (b, far)
    peers = [sibling, beside, (up, o), (up, far), (down, o), (down, far)]

    def op_copy(k):
        return pltpu.make_async_copy(ops.at[k], stage.at[k, pl.ds(0, F)], op_sem.at[k])

    barrier = pltpu.get_barrier_semaphore()
    for peer in peers:
        pl.semaphore_signal(barrier, inc=1, device_id=peer, device_id_type=MESH)
    pairs = ((den_hbm, den), (ocnt_hbm, ocnt), (gcnt_hbm, gcnt), (tgt_hbm, tgt), (src_hbm, src))
    inputs = [pltpu.make_async_copy(a, v, in_sem.at[i]) for i, (a, v) in enumerate(pairs)]
    for c in inputs:
        c.start()
    for k in range(OFFS):
        op_copy(k).start()
    inputs[0].wait()

    me = 4 + o
    for lt in range(3):
        parts = [den[8 * (lt + 3 * g) : 8 * (lt + 3 * g) + 8, 256:F] for g in range(3)]
        rx[me, lt] = jnp.concatenate([*parts, jnp.zeros((8, 8), F32)], axis=1)
    for rt in range(9):
        for h in range(2):
            rx[me, 3 + 2 * rt + h] = den[8 * rt : 8 * rt + 8, 128 * h : 128 * h + 128]

    for c in inputs[1:]:
        c.wait()
    counts_o, counts_g = ocnt[...], gcnt[...]
    os0, os1, os2 = (start_at(counts_o, b + i) for i in (-1, 0, 1))
    gs1, gs2 = (start_at(counts_g, b + i) for i in (0, 1))
    shift = gs1 - os1
    m = src[0]
    before, own = m - os0, m - os1
    before = 512 + jnp.where(before < 256, before, before - 256)
    own = jnp.where(own < 256, own, own + 192)
    place = jnp.where(m < os1, before, jnp.where(m < os2, own, 256 + m - os2))
    place = jnp.where(tgt[0] < CAP, place, -1)
    j = iota((CAP, 384), 0) + shift
    j = jnp.where(j < 0, j + CAP, jnp.where(j >= CAP, j - CAP, j))
    turn = jnp.where(j == slot_of_column(iota((CAP, 384), 1)), 1.0, 0.0).astype(F32)
    turned = jnp.dot(place.astype(F32), turn, precision=lax.Precision.HIGHEST, preferred_element_type=F32)
    turned = (turned + 0.25 * jnp.where(turned < 0, -1.0, 1.0)).astype(I32)
    pmain[...] = turned[:, :256]
    lane_id = iota((1, 128), 1)
    group_of_lane = lane_id >> 5
    for t in range(2):
        rows = []
        for h in range(2):
            row = jnp.zeros((1, 128), I32)
            for a in range(4):
                k = 8 * t + 4 * h + a
                row = jnp.where(group_of_lane == a, turned[k : k + 1, 256:384], row)
            rows.append(row)
        pleft[t : t + 1] = jnp.concatenate(rows, axis=1)

    s = slot_of_column(iota((384, 128), 0))
    real = iota((384, 128), 0) < CAP
    lane = iota((384, 128), 1)
    is_head = real & (s >= CAP - EDGE) & (os1 + s - CAP >= gs1) & (s - (CAP - EDGE) == lane)
    box1 = os1 + s
    tail = jnp.where((box1 >= os2) & (box1 < gs2), box1 - os2, jnp.where(box1 + CAP < gs2, box1 + CAP - os2, -1))
    hot_send[:, :128] = jnp.where(is_head, 1.0, 0.0).astype(BF16)
    hot_send[:, 128:] = jnp.where(real & (tail == lane), 1.0, 0.0).astype(BF16)
    r = iota((256, 128), 0)
    slot = jnp.where(r < 128, os2 - os1 + r - EDGE, r - 128)
    known = jnp.where(r < 128, r, r - 128) < EDGE
    lane = iota((256, 128), 1)
    hot_recv[:, :128] = jnp.where(known & (slot == slot_of_column(lane + 128 * chip)), 1.0, 0.0).astype(BF16)
    hot_recv[:, 128:] = jnp.where(known & (lane < 32) & (slot == slot_of_column(lane + 256)), 1.0, 0.0).astype(BF16)

    def block_copy(here, there, count, send, device):
        return pltpu.make_async_remote_copy(
            src_ref=rx.at[here, pl.ds(0, count)], dst_ref=rx.at[there, pl.ds(0, count)],
            send_sem=send, recv_sem=rsem.at[there], device_id=device, device_id_type=MESH,
        )

    pl.semaphore_wait(barrier, len(peers))

    def to_prev_segment(i):
        return block_copy(me, o, TILES, ici_send.at[1 + i], peers[2 + i])

    def to_next_segment(i, count):
        return block_copy(me, 8 + o, count, ici_send.at[3 + i], peers[4 + i])

    to_beside = block_copy(me, me, TILES, ici_send.at[0], beside)
    to_sibling = block_copy(me, me, TILES, sib_send.at[0], sibling)
    for i in (1, 0):
        to_prev_segment(i).start()

        @pl.when(o < 2)
        def _():
            to_next_segment(i, TILES).start()

        @pl.when(o == 2)
        def _():
            to_next_segment(i, SHORT).start()

    to_beside.start()
    to_sibling.start()

    stage[:, pl.ds(F, 8), :] = jnp.zeros((OFFS, 8, F), F32)

    def split_pair(q, _):
        for par in range(2):
            k = 2 * q + par
            op_copy(k).wait()
            v = stage[k]
            hi = v.astype(BF16)
            hi32 = hi.astype(F32)
            lo32 = v - hi32
            o_main[q, :304, 256 * par : 256 * par + 256] = hi[:, :256]
            o_main[q, 304:, 256 * par : 256 * par + 256] = lo32[:, :256].astype(BF16)
            last = jnp.concatenate([hi32[:, 256:], hi32[:, 256:], lo32[:, 256:], jnp.zeros((304, 8), F32)], axis=1)
            o_left[q, :, 128 * par : 128 * par + 128] = last.astype(BF16)
        return 0

    def arrived(there, count=TILES):
        block_copy(there, there, count, ici_send.at[0], sibling).wait_recv()

    def hand_on(i, there, count=TILES):
        return block_copy(there, there, count, sib_send.at[i], sibling)

    def pass_own():
        arrived(4 + far)
        hand_on(1, 4 + far).start()

    def pass_prev():
        for i, there in ((2, o), (3, far)):
            arrived(there)
            hand_on(i, there).start()

    def pass_next():
        arrived(8 + core)
        hand_on(4, 8 + core).start()

        @pl.when(core == 0)
        def _():
            arrived(10, SHORT)
            hand_on(5, 10, SHORT).start()

    def row_tiles(segment, tiles):
        return [(4 * segment + r // 9, r % 9) for r in tiles]

    def wide_left(idx, rt):
        left = rx[idx, rt % 3]
        return rx[idx, 3 + 2 * rt], rx[idx, 4 + 2 * rt], pltpu.roll(left, 128 - 40 * (rt // 3), 1) if rt >= 3 else left

    def turn_rows(t, half, parts):
        cols = [jnp.concatenate(list(p), axis=0).T for p in zip(*parts)]
        v = jnp.concatenate([cols[0], cols[1], cols[2][:40]], axis=0)
        hi32 = v.astype(BF16).astype(F32)
        lo32 = v - hi32
        xt[t, :, 128 * half : 128 * half + 128] = jnp.concatenate(
            [hi32[:256], lo32[:256], hi32[256:F], lo32[256:F]], axis=0
        ).astype(BF16)

    def turn_own():
        for half in range(2):
            turn_rows(0, half, [wide_left(*a) for a in row_tiles(1, range(16 * half, 16 * half + 16))])

    def turn_next():
        turn_rows(1, 0, [wide_left(*a) for a in row_tiles(2, range(16))])
        parts = [wide_left(*a) for a in row_tiles(2, range(16, 24)) + row_tiles(1, range(32, 36))]
        turn_rows(1, 1, parts + [(jnp.zeros((8, 128), F32),) * 3] * 4)

    def turn_prev():
        parts = [wide_left(*a) for a in row_tiles(0, range(16))]
        folded = [wide_left(*a) for a in row_tiles(0, range(32, 36))]
        long = os1 - os0 > 256
        for r in range(4):
            parts[r] = tuple(jnp.where(long, x, y) for x, y in zip(folded[r], parts[r]))
        turn_rows(2, 0, parts)
        turn_rows(2, 1, [wide_left(*a) for a in row_tiles(0, range(16, 32))])

    def gathered(row, t):
        hot = jnp.where(iota((256, 256), 0) + 256 * t == row, 1.0, 0.0).astype(BF16)
        return jnp.dot(xt[t], hot, preferred_element_type=F32)

    def put(q, par, columns, g, add):
        tail = jnp.concatenate([g[512:592], g[512:552], jnp.zeros((8, g.shape[1]), F32)], axis=0)
        for ref, at, v in (
            (g_hi, pl.ds(256 * par, 256), g[:256]),
            (g_lo, pl.ds(256 * par, 256), g[256:512]),
            (g_last, pl.ds(128 * par, 128), tail),
        ):
            v = v.astype(BF16)
            ref[q, at, columns] = ref[q, at, columns] + v if add else v

    def gather(t, add):
        def gather_pair(q, _):
            for par in range(2):
                put(q, par, pl.ds(0, 256), gathered(pmain[pl.ds(2 * q + par, 1), :], t), add)
            return 0

        lax.fori_loop(0, OFFS // 2, gather_pair, 0)

        def gather_left(i, _):
            g = gathered(pleft[pl.ds(i, 1), :], t)
            for kk in range(8):
                h, a = kk // 4, kk % 4
                part = jnp.where(group_of_lane == a, g[:, 128 * h : 128 * h + 128], 0.0)
                put(4 * i + kk // 2, kk % 2, pl.ds(256, 128), part, add)
            return 0

        lax.fori_loop(0, 2, gather_left, 0)

    lax.fori_loop(0, OFFS // 4, split_pair, 0)
    pass_own()
    lax.fori_loop(OFFS // 4, OFFS // 2, split_pair, 0)
    even = b % 2 == 0
    pl.when(even)(pass_next)
    odd = jnp.logical_not(even)
    pl.when(odd)(pass_prev)

    def took_prev():
        arrived(sib)
        arrived((sib + 2) % 4)
        turn_prev()

    def took_next():
        arrived(9 - core)

        @pl.when(core == 1)
        def _():
            arrived(10, SHORT)

        turn_next()

    arrived(4 + sib)
    arrived(4 + (sib + 2) % 4)
    turn_own()
    gather(0, False)
    pl.when(even)(pass_prev)
    pl.when(odd)(pass_next)
    pl.when(even)(took_next)
    pl.when(odd)(took_prev)
    gather(jnp.where(even, 1, 2), True)
    pl.when(even)(took_prev)
    pl.when(odd)(took_next)
    gather(jnp.where(even, 2, 1), True)

    def product(q, at):
        both = jnp.dot(o_main[q], g_hi[q, :, at], preferred_element_type=F32)
        third = jnp.dot(o_main[q, :304], g_lo[q, :, at], preferred_element_type=F32)
        return both[:304] + both[304:] + third + jnp.dot(o_left[q], g_last[q, :, at], preferred_element_type=F32)

    def multiply(ref, at, first, last):
        def step(q, _):
            ref[...] += product(q, at)
            return 0

        lax.fori_loop(first, last, step, 0)

    main, side = slice(0, 256), slice(256, 384)
    acc[...] = product(0, main)
    multiply(acc, main, 1, OFFS // 2)

    def packed(half):
        v = ufold[pl.ds(pl.multiple_of(STEP * half, 8), 160), :]
        row = jnp.zeros((40, 128), F32)
        for a in range(4):
            row = jnp.where(group_of_lane == a, v[40 * a : 40 * a + 40], row)
        return row

    def unpacked(v):
        parts = [v if a == 0 else pltpu.roll(v, 128 - 32 * a, 1) for a in range(4)]
        return jnp.concatenate(parts, axis=0)[:HALF]

    def send(i, source, target, device, recv=None):
        return pltpu.make_async_remote_copy(
            src_ref=source, dst_ref=target, send_sem=osend.at[i], recv_sem=orecv.at[i if recv is None else recv],
            device_id=device, device_id_type=MESH,
        )

    theirs = pl.ds(pl.multiple_of(STEP * (1 - core), 8), HALF)
    mine = pl.ds(pl.multiple_of(STEP * core, 8), HALF)
    swap = [send(0, acc.at[theirs], ra, sibling), send(1, lpack, ral, sibling)]
    cross = [send(2, q_ref.at[1 - chip], rq, beside), send(3, ql_ref, rql, beside)]
    swap[0].start()
    ufold[...] = product(0, side)
    multiply(ufold, side, 1, 4)
    swap[0].wait_recv()
    q_ref[0] = acc[mine, :128] + ra[:, :128]
    q_ref[1] = acc[mine, 128:] + ra[:, 128:]
    cross[0].start()
    multiply(ufold, side, 4, OFFS // 2)
    u = ufold[...]
    u = u + pltpu.roll(u, 64, 1)
    ufold[...] = u + pltpu.roll(u, 32, 1)
    lpack[...] = packed(1 - core)
    swap[1].start()
    own_left = packed(core)
    hi, lo = split(jnp.concatenate([q_ref[0], q_ref[1]], axis=1))
    edges = jnp.dot(hi, hot_send[:256], preferred_element_type=F32)
    edges = edges + jnp.dot(lo, hot_send[:256], preferred_element_type=F32)
    swap[1].wait_recv()
    ql = own_left + ral[...]
    ql_ref[...] = ql
    cross[1].start()
    hi, lo = split(unpacked(ql))
    edges = edges + jnp.dot(hi, hot_send[256:], preferred_element_type=F32)
    edges = edges + jnp.dot(lo, hot_send[256:], preferred_element_type=F32)
    for i in range(2):
        e = jnp.concatenate([edges[:, 128 * i : 128 * i + 128], jnp.zeros((8, 128), F32)], axis=0)
        for a in range(3):
            ht[i, 40 * a : 40 * a + 40] = e[40 * a : 40 * a + 40] + jnp.where(
                lane_id >= EDGE, pltpu.roll(e[120:160], 96 - 32 * a, 1), 0.0
            )
    heads = [send(4 + i, ht.at[0], hr.at[chip], peers[4 + i], 4 + chip) for i in range(2)]
    tails = send(6, ht.at[1], tr.at[chip], (up, core), 6 + chip)
    for c in (heads[1], tails, heads[0]):
        c.start()
    for c in cross:
        c.wait_recv()
    s = slot_of_column(iota((1, 128), 1) + 128 * chip)
    box1 = os1 + s
    keep = (box1 >= gs1) & (box1 < gs2) & (box1 < os2)
    own = jnp.where(keep, q_ref[chip] + rq[...], 0.0)
    box1 = os1 + slot_of_column(256 + (iota((1, 128), 1) & 31))
    keep = (box1 >= gs1) & (box1 < gs2) & (box1 < os2)
    own_left = unpacked(jnp.where(keep, ql_ref[...] + rql[...], 0.0))
    for i in range(2):
        send(4 + i, ht.at[0], hr.at[i], peers[4], 4 + i).wait_recv()

    @pl.when(chip == 0)
    def _():
        for i in range(2):
            send(6, ht.at[1], tr.at[i], peers[4], 6 + i).wait_recv()

    @pl.when(chip == 1)
    def _():
        tr[...] = jnp.zeros(tr.shape, F32)

    def edge_rows(v):
        thirds = [pltpu.roll(v[40 * a : 40 * a + 40], 32 * a + 32, 1) for a in range(3)]
        quarter = jnp.where(lane_id < 32, thirds[0], jnp.where(lane_id < 64, thirds[1], thirds[2]))
        return jnp.concatenate([v, quarter], axis=0)[:HALF]

    hi, lo = split(jnp.concatenate([edge_rows(hr[0] + hr[1]), edge_rows(tr[0] + tr[1])], axis=1))
    moved = jnp.dot(hi, hot_recv[...], preferred_element_type=F32) + jnp.dot(
        lo, hot_recv[...], preferred_element_type=F32
    )
    v0, v1 = own + moved[:, :128], own_left + moved[:, 128:]
    v_ref[0], v_ref[1] = v0, v1
    last = send(8, v_ref, fr, sibling)
    last.start()
    for i, v in enumerate((v0, v1)):
        fin[i, mine] = v
    last.wait_recv()
    for i in range(2):
        fin[i, theirs] = fr[i]
        tt[i] = fin[i].T
    out[0:64] = tt[0, pl.ds(pl.multiple_of(64 * core, 8), 64), :F]
    out[64:72] = tt[1, pl.ds(pl.multiple_of(8 * o, 8), 8), :F]

    for c in (to_beside, to_sibling, *(to_prev_segment(i) for i in range(2))):
        c.wait_send()
    for i, there in enumerate((4 + far, o, far, 8 + core)):
        hand_on(1 + i, there).wait_send()

    @pl.when(core == 0)
    def _():
        hand_on(5, 10, SHORT).wait_send()

    @pl.when(o < 2)
    def _():
        for i in range(2):
            to_next_segment(i, TILES).wait_send()

    @pl.when(o == 2)
    def _():
        for i in range(2):
            to_next_segment(i, SHORT).wait_send()

    for c in (*swap, *cross, *heads, tails, last):
        c.wait_send()


def body(density, operators, owner_count, group_count, target_slot, source_box):
    vmem = pl.BlockSpec(memory_space=pltpu.VMEM)
    scratch = [
        pltpu.VMEM((ROWS, F), F32),
        pltpu.VMEM(owner_count[None].shape, I32),
        pltpu.VMEM(group_count[None].shape, I32),
        pltpu.VMEM((1, OFFS, CAP), I32),
        pltpu.VMEM((1, OFFS, CAP), I32),
        pltpu.VMEM((12, TILES, 8, 128), F32),
        pltpu.VMEM((OFFS, 304, F), F32),
        pltpu.VMEM((OFFS // 2, 608, 512), BF16),
        pltpu.VMEM((OFFS // 2, 304, 256), BF16),
        pltpu.VMEM((3, 592, 256), BF16),
        pltpu.VMEM((OFFS, 256), I32),
        pltpu.VMEM((2, 256), I32),
        pltpu.VMEM((OFFS // 2, 512, 384), BF16),
        pltpu.VMEM((OFFS // 2, 512, 384), BF16),
        pltpu.VMEM((OFFS // 2, 256, 384), BF16),
        pltpu.VMEM((304, 256), F32),
        pltpu.VMEM((304, 128), F32),
        pltpu.VMEM((384, 256), BF16),
        pltpu.VMEM((256, 256), BF16),
        pltpu.VMEM((40, 128), F32),
        pltpu.VMEM((HALF, 256), F32),
        pltpu.VMEM((40, 128), F32),
        pltpu.VMEM((2, HALF, 128), F32),
        pltpu.VMEM((40, 128), F32),
        pltpu.VMEM((2, 120, 128), F32),
        pltpu.VMEM((HALF, 128), F32),
        pltpu.VMEM((40, 128), F32),
        pltpu.VMEM((2, 120, 128), F32),
        pltpu.VMEM((2, 120, 128), F32),
        pltpu.VMEM((2, HALF, 128), F32),
        pltpu.VMEM((2, HALF, 128), F32),
        pltpu.VMEM((2, 384, 128), F32),
        pltpu.VMEM((2, 128, 384), F32),
        pltpu.SemaphoreType.DMA((5,)),
        pltpu.SemaphoreType.DMA((OFFS,)),
        pltpu.SemaphoreType.DMA((5,)),
        pltpu.SemaphoreType.DMA((6,)),
        pltpu.SemaphoreType.DMA((12,)),
        pltpu.SemaphoreType.DMA((9,)),
        pltpu.SemaphoreType.DMA((9,)),
    ]
    return pl.pallas_call(
        kernel,
        out_shape=jax.ShapeDtypeStruct((ROWS, F), F32),
        in_specs=[pl.BlockSpec(memory_space=pltpu.HBM)] * 6,
        out_specs=vmem,
        scratch_shapes=scratch,
        compiler_params=pltpu.CompilerParams(
            collective_id=0, has_side_effects=True, vmem_limit_bytes=60 * 2**20
        ),
        name="translate",
    )(density, operators, owner_count[None], group_count[None], target_slot, source_box)


def solution(mesh):
    placed = (P(("box", "op"), None), P("op", None, None), P(), P(), P("box", "op", None), P("box", "op", None))
    return jax.shard_map(
        body, mesh=mesh, in_specs=placed, out_specs=P(("box", "op"), None), check_vma=False
    )
```

```python
import jax
import jax.numpy as jnp
from jax import lax
from jax.experimental import pallas as pl
from jax.experimental.pallas import tpu as pltpu
from jax.sharding import PartitionSpec as P

MESH = pl.DeviceIdType.MESH
F32, BF16, I32 = jnp.float32, jnp.bfloat16, jnp.int32
ROWS = 72
CAP = 288
EDGE = 96
F = 296
HALF = 152
STEP = 144
OFFS = 16
TILES = 21
SHORT = 15


def iota(shape, dim):
    return lax.broadcasted_iota(I32, shape, dim)


def split(v):
    hi = v.astype(BF16)
    lo = (v - hi.astype(F32)).astype(BF16)
    return hi, lo


def slot_of_column(col):
    main = 72 * (col >> 6) + (col & 63)
    c = col & 31
    left = 72 * (c >> 3) + 64 + (c & 7)
    return jnp.where(col < 256, main, left)


def start_at(counts, index):
    lane = iota(counts.shape, 1)
    return jnp.sum(jnp.where(lane < index, counts.astype(F32), 0.0), axis=1, keepdims=True).astype(I32)


def kernel(
    den_hbm, ops, ocnt_hbm, gcnt_hbm, tgt_hbm, src_hbm, out,
    den, ocnt, gcnt, tgt, src, rx, stage, o_main, o_left, xt, pmain, pleft, g_both, g_lo, g_last, acc, side, ufold,
    hot_send, hot_recv, lpack, ra, ral, q_ref, ql_ref, ht, rq, rql, hr, tr, v_ref, fr, fin, tt,
    in_sem, op_sem, ici_send, sib_send, rsem, osend, orecv,
):
    b, o = lax.axis_index("box"), lax.axis_index("op")
    n = lax.axis_size("box")
    core, chip = o % 2, o // 2
    far, sib = (o + 2) % 4, o + 1 - 2 * core
    up, down = (b + 1) % n, (b + n - 1) % n
    sibling, beside = (b, sib), (b, far)
    peers = [sibling, beside, (up, o), (up, far), (down, o), (down, far)]

    def op_copy(k):
        return pltpu.make_async_copy(ops.at[k], stage.at[k, pl.ds(0, F)], op_sem.at[k])

    barrier = pltpu.get_barrier_semaphore()
    for peer in peers:
        pl.semaphore_signal(barrier, inc=1, device_id=peer, device_id_type=MESH)
    pairs = ((den_hbm, den), (ocnt_hbm, ocnt), (gcnt_hbm, gcnt), (tgt_hbm, tgt), (src_hbm, src))
    inputs = [pltpu.make_async_copy(a, v, in_sem.at[i]) for i, (a, v) in enumerate(pairs)]
    for c in inputs:
        c.start()
    for k in range(OFFS):
        op_copy(k).start()
    inputs[0].wait()

    me = 4 + o
    for lt in range(3):
        parts = [den[8 * (lt + 3 * g) : 8 * (lt + 3 * g) + 8, 256:F] for g in range(3)]
        rx[me, lt] = jnp.concatenate([*parts, jnp.zeros((8, 8), F32)], axis=1)
    for rt in range(9):
        for h in range(2):
            rx[me, 3 + 2 * rt + h] = den[8 * rt : 8 * rt + 8, 128 * h : 128 * h + 128]

    for c in inputs[1:]:
        c.wait()
    counts_o, counts_g = ocnt[...], gcnt[...]
    os0, os1, os2 = (start_at(counts_o, b + i) for i in (-1, 0, 1))
    gs1, gs2 = (start_at(counts_g, b + i) for i in (0, 1))
    shift = gs1 - os1
    m = src[0]
    before, own = m - os0, m - os1
    before = 512 + jnp.where(before < 256, before, before - 256)
    own = jnp.where(own < 256, own, own + 192)
    place = jnp.where(m < os1, before, jnp.where(m < os2, own, 256 + m - os2))
    place = jnp.where(tgt[0] < CAP, place, -1)
    j = iota((CAP, 384), 0) + shift
    j = jnp.where(j < 0, j + CAP, jnp.where(j >= CAP, j - CAP, j))
    turn = jnp.where(j == slot_of_column(iota((CAP, 384), 1)), 1.0, 0.0).astype(F32)
    turned = jnp.dot(place.astype(F32), turn, precision=lax.Precision.HIGHEST, preferred_element_type=F32)
    turned = (turned + 0.25 * jnp.where(turned < 0, -1.0, 1.0)).astype(I32)
    lane_id = iota((1, 128), 1)
    group_of_lane = lane_id >> 5
    for i in range(4):
        pmain[i : i + 1] = jnp.concatenate([turned[k : k + 1, :256] for k in range(4 * i, 4 * i + 4)], axis=1)
        row = jnp.zeros((1, 128), I32)
        for a in range(4):
            row = jnp.where(group_of_lane == a, turned[4 * i + a : 4 * i + a + 1, 256:384], row)
        pleft[:, 128 * i : 128 * i + 128] = row

    s = slot_of_column(iota((384, 128), 0))
    real = iota((384, 128), 0) < CAP
    lane = iota((384, 128), 1)
    is_head = real & (s >= CAP - EDGE) & (os1 + s - CAP >= gs1) & (s - (CAP - EDGE) == lane)
    box1 = os1 + s
    tail = jnp.where((box1 >= os2) & (box1 < gs2), box1 - os2, jnp.where(box1 + CAP < gs2, box1 + CAP - os2, -1))
    hot_send[:, :128] = jnp.where(is_head, 1.0, 0.0).astype(BF16)
    hot_send[:, 128:] = jnp.where(real & (tail == lane), 1.0, 0.0).astype(BF16)
    r = iota((256, 128), 0)
    slot = jnp.where(r < 128, os2 - os1 + r - EDGE, r - 128)
    known = jnp.where(r < 128, r, r - 128) < EDGE
    lane = iota((256, 128), 1)
    hot_recv[:, :128] = jnp.where(known & (slot == slot_of_column(lane + 128 * chip)), 1.0, 0.0).astype(BF16)
    hot_recv[:, 128:] = jnp.where(known & (lane < 32) & (slot == slot_of_column(lane + 256)), 1.0, 0.0).astype(BF16)

    def block_copy(here, there, count, send, device):
        return pltpu.make_async_remote_copy(
            src_ref=rx.at[here, pl.ds(0, count)], dst_ref=rx.at[there, pl.ds(0, count)],
            send_sem=send, recv_sem=rsem.at[there], device_id=device, device_id_type=MESH,
        )

    pl.semaphore_wait(barrier, len(peers))

    def to_prev_segment(i):
        return block_copy(me, o, TILES, ici_send.at[1 + i], peers[2 + i])

    def to_next_segment(i, count):
        return block_copy(me, 8 + o, count, ici_send.at[3 + i], peers[4 + i])

    to_beside = block_copy(me, me, TILES, ici_send.at[0], beside)
    to_sibling = block_copy(me, me, TILES, sib_send.at[0], sibling)
    for i in (1, 0):
        to_prev_segment(i).start()

        @pl.when(o < 2)
        def _():
            to_next_segment(i, TILES).start()

        @pl.when(o == 2)
        def _():
            to_next_segment(i, SHORT).start()

    to_beside.start()
    to_sibling.start()

    stage[:, pl.ds(F, 8), :] = jnp.zeros((OFFS, 8, F), F32)

    def split_eight(q, _):
        for a in range(8):
            k = 8 * q + a
            op_copy(k).wait()
            v = stage[k]
            hi = v.astype(BF16)
            hi32 = hi.astype(F32)
            lo32 = v - hi32
            o_main[q, :304, 256 * a : 256 * a + 256] = hi[:, :256]
            o_main[q, 304:, 256 * a : 256 * a + 256] = lo32[:, :256].astype(BF16)
            last = jnp.concatenate([hi32[:, 256:], hi32[:, 256:], lo32[:, 256:], jnp.zeros((304, 8), F32)], axis=1)
            o_left[q, :, 128 * a : 128 * a + 128] = last.astype(BF16)
        return 0

    def arrived(there, count=TILES):
        block_copy(there, there, count, ici_send.at[0], sibling).wait_recv()

    def hand_on(i, there, count=TILES):
        return block_copy(there, there, count, sib_send.at[i], sibling)

    def pass_own():
        arrived(4 + far)
        hand_on(1, 4 + far).start()

    def pass_prev():
        for i, there in ((2, o), (3, far)):
            arrived(there)
            hand_on(i, there).start()

    def pass_next():
        arrived(8 + core)
        hand_on(4, 8 + core).start()

        @pl.when(core == 0)
        def _():
            arrived(10, SHORT)
            hand_on(5, 10, SHORT).start()

    def row_tiles(segment, tiles):
        return [(4 * segment + r // 9, r % 9) for r in tiles]

    def wide_left(idx, rt):
        left = rx[idx, rt % 3]
        return rx[idx, 3 + 2 * rt], rx[idx, 4 + 2 * rt], pltpu.roll(left, 128 - 40 * (rt // 3), 1) if rt >= 3 else left

    def turn_rows(t, half, parts):
        cols = [jnp.concatenate(list(p), axis=0).T for p in zip(*parts)]
        v = jnp.concatenate([cols[0], cols[1], cols[2][:40]], axis=0)
        hi32 = v.astype(BF16).astype(F32)
        lo32 = v - hi32
        xt[t, :, 128 * half : 128 * half + 128] = jnp.concatenate(
            [hi32[:256], lo32[:256], hi32[256:F], lo32[256:F]], axis=0
        ).astype(BF16)

    def turn_own():
        for half in range(2):
            turn_rows(0, half, [wide_left(*a) for a in row_tiles(1, range(16 * half, 16 * half + 16))])

    def turn_next():
        turn_rows(1, 0, [wide_left(*a) for a in row_tiles(2, range(16))])
        parts = [wide_left(*a) for a in row_tiles(2, range(16, 24)) + row_tiles(1, range(32, 36))]
        turn_rows(1, 1, parts + [(jnp.zeros((8, 128), F32),) * 3] * 4)

    def turn_prev():
        parts = [wide_left(*a) for a in row_tiles(0, range(16))]
        folded = [wide_left(*a) for a in row_tiles(0, range(32, 36))]
        long = os1 - os0 > 256
        for r in range(4):
            parts[r] = tuple(jnp.where(long, x, y) for x, y in zip(folded[r], parts[r]))
        turn_rows(2, 0, parts)
        turn_rows(2, 1, [wide_left(*a) for a in row_tiles(0, range(16, 32))])

    def gathered(row, t):
        rows = xt[0] if t == 0 else jnp.concatenate([xt[1], xt[2]], axis=1)
        hot = jnp.where(iota((rows.shape[1], row.shape[1]), 0) + 256 * t == row, 1.0, 0.0).astype(BF16)
        return jnp.dot(rows, hot, preferred_element_type=F32)

    def put(q, a, g, left, add):
        tail = jnp.concatenate([g[512:592], g[512:552], jnp.zeros((8, g.shape[1]), F32)], axis=0)
        rows, short = pl.ds(256 * a, 256), pl.ds(128 * a, 128)
        for ref, at, columns, v in (
            (g_both, rows, pl.ds(256, 128) if left else pl.ds(0, 256), g[:256]),
            (g_both, rows, pl.ds(384, 128), g[256:512]) if left else (g_lo, rows, pl.ds(0, 256), g[256:512]),
            (g_last, short, pl.ds(256, 128) if left else pl.ds(0, 256), tail),
        ):
            v = v.astype(BF16)
            ref[q, at, columns] = ref[q, at, columns] + v if add else v

    def gather(t, add):
        def gather_eight(q, _):
            for h in range(2):
                g = gathered(pmain[pl.ds(2 * q + h, 1), :], t)
                for a in range(4):
                    put(q, 4 * h + a, g[:, 256 * a : 256 * a + 256], False, add)
            return 0

        lax.fori_loop(0, 2, gather_eight, 0)
        g = gathered(pleft[...], t)
        for k in range(OFFS):
            part = g[:, 128 * (k // 4) : 128 * (k // 4) + 128]
            put(k // 8, k % 8, jnp.where(group_of_lane == k % 4, part, 0.0), True, add)

    lax.fori_loop(0, 1, split_eight, 0)
    pass_own()
    lax.fori_loop(1, 2, split_eight, 0)
    even = b % 2 == 0
    pl.when(even)(pass_next)
    odd = jnp.logical_not(even)
    pl.when(odd)(pass_prev)

    pl.when(even)(pass_prev)
    pl.when(odd)(pass_next)
    arrived(4 + sib)
    arrived(4 + (sib + 2) % 4)
    turn_own()
    gather(0, False)
    for there in (sib, (sib + 2) % 4, 9 - core):
        arrived(there)

    @pl.when(core == 1)
    def _():
        arrived(10, SHORT)

    turn_next()
    turn_prev()
    gather(1, True)

    acc[...] = jnp.zeros(acc.shape, F32)
    side[...] = jnp.zeros(side.shape, F32)

    def multiply(q, _):
        both = jnp.dot(o_main[q], g_both[q], preferred_element_type=F32)
        third = jnp.dot(o_main[q, :304], g_lo[q], preferred_element_type=F32)
        last = jnp.dot(o_left[q], g_last[q], preferred_element_type=F32)
        both = both[:304] + both[304:]
        acc[...] += both[:, :256] + third + last[:, :256]
        side[...] += both[:, 256:384] + both[:, 384:] + last[:, 256:]
        return 0

    lax.fori_loop(0, 2, multiply, 0)

    def packed(half):
        v = ufold[pl.ds(pl.multiple_of(STEP * half, 8), 160), :]
        row = jnp.zeros((40, 128), F32)
        for a in range(4):
            row = jnp.where(group_of_lane == a, v[40 * a : 40 * a + 40], row)
        return row

    def unpacked(v):
        parts = [v if a == 0 else pltpu.roll(v, 128 - 32 * a, 1) for a in range(4)]
        return jnp.concatenate(parts, axis=0)[:HALF]

    def send(i, source, target, device, recv=None):
        return pltpu.make_async_remote_copy(
            src_ref=source, dst_ref=target, send_sem=osend.at[i], recv_sem=orecv.at[i if recv is None else recv],
            device_id=device, device_id_type=MESH,
        )

    theirs = pl.ds(pl.multiple_of(STEP * (1 - core), 8), HALF)
    mine = pl.ds(pl.multiple_of(STEP * core, 8), HALF)
    swap = [send(0, acc.at[theirs], ra, sibling), send(1, lpack, ral, sibling)]
    swap[0].start()
    u = side[...]
    u = u + pltpu.roll(u, 64, 1)
    ufold[...] = u + pltpu.roll(u, 32, 1)
    lpack[...] = packed(1 - core)
    swap[1].start()
    own_left = packed(core)
    for c in swap:
        c.wait_recv()
    q0 = acc[mine, :128] + ra[:, :128]
    q1 = acc[mine, 128:256] + ra[:, 128:]
    ql = own_left + ral[...]
    q_ref[0], q_ref[1], ql_ref[...] = q0, q1, ql
    cross = [send(2, q_ref.at[1 - chip], rq, beside), send(3, ql_ref, rql, beside)]
    for c in cross:
        c.start()
    hi, lo = split(jnp.concatenate([q0, q1, unpacked(ql)], axis=1))
    edges = jnp.dot(hi, hot_send[...], preferred_element_type=F32)
    edges = edges + jnp.dot(lo, hot_send[...], preferred_element_type=F32)
    for i in range(2):
        e = jnp.concatenate([edges[:, 128 * i : 128 * i + 128], jnp.zeros((8, 128), F32)], axis=0)
        for a in range(3):
            ht[i, 40 * a : 40 * a + 40] = e[40 * a : 40 * a + 40] + jnp.where(
                lane_id >= EDGE, pltpu.roll(e[120:160], 96 - 32 * a, 1), 0.0
            )
    heads = [send(4 + i, ht.at[0], hr.at[chip], peers[4 + i], 4 + chip) for i in range(2)]
    tails = send(6, ht.at[1], tr.at[chip], (up, core), 6 + chip)
    for c in (heads[1], tails, heads[0]):
        c.start()
    for c in cross:
        c.wait_recv()
    s = slot_of_column(iota((1, 128), 1) + 128 * chip)
    box1 = os1 + s
    keep = (box1 >= gs1) & (box1 < gs2) & (box1 < os2)
    own = jnp.where(keep, q_ref[chip] + rq[...], 0.0)
    box1 = os1 + slot_of_column(256 + (iota((1, 128), 1) & 31))
    keep = (box1 >= gs1) & (box1 < gs2) & (box1 < os2)
    own_left = unpacked(jnp.where(keep, ql_ref[...] + rql[...], 0.0))
    for i in range(2):
        send(4 + i, ht.at[0], hr.at[i], peers[4], 4 + i).wait_recv()

    @pl.when(chip == 0)
    def _():
        for i in range(2):
            send(6, ht.at[1], tr.at[i], peers[4], 6 + i).wait_recv()

    @pl.when(chip == 1)
    def _():
        tr[...] = jnp.zeros(tr.shape, F32)

    def edge_rows(v):
        thirds = [pltpu.roll(v[40 * a : 40 * a + 40], 32 * a + 32, 1) for a in range(3)]
        quarter = jnp.where(lane_id < 32, thirds[0], jnp.where(lane_id < 64, thirds[1], thirds[2]))
        return jnp.concatenate([v, quarter], axis=0)[:HALF]

    hi, lo = split(jnp.concatenate([edge_rows(hr[0] + hr[1]), edge_rows(tr[0] + tr[1])], axis=1))
    moved = jnp.dot(hi, hot_recv[...], preferred_element_type=F32) + jnp.dot(
        lo, hot_recv[...], preferred_element_type=F32
    )
    v0, v1 = own + moved[:, :128], own_left + moved[:, 128:]
    v_ref[0], v_ref[1] = v0, v1
    last = send(8, v_ref, fr, sibling)
    last.start()
    for i, v in enumerate((v0, v1)):
        fin[i, mine] = v
    last.wait_recv()
    for i in range(2):
        fin[i, theirs] = fr[i]
        tt[i] = fin[i].T
    out[0:64] = tt[0, pl.ds(pl.multiple_of(64 * core, 8), 64), :F]
    out[64:72] = tt[1, pl.ds(pl.multiple_of(8 * o, 8), 8), :F]

    for c in (to_beside, to_sibling, *(to_prev_segment(i) for i in range(2))):
        c.wait_send()
    for i, there in enumerate((4 + far, o, far, 8 + core)):
        hand_on(1 + i, there).wait_send()

    @pl.when(core == 0)
    def _():
        hand_on(5, 10, SHORT).wait_send()

    @pl.when(o < 2)
    def _():
        for i in range(2):
            to_next_segment(i, TILES).wait_send()

    @pl.when(o == 2)
    def _():
        for i in range(2):
            to_next_segment(i, SHORT).wait_send()

    for c in (*swap, *cross, *heads, tails, last):
        c.wait_send()


def body(density, operators, owner_count, group_count, target_slot, source_box):
    vmem = pl.BlockSpec(memory_space=pltpu.VMEM)
    scratch = [
        pltpu.VMEM((ROWS, F), F32),
        pltpu.VMEM(owner_count[None].shape, I32),
        pltpu.VMEM(group_count[None].shape, I32),
        pltpu.VMEM((1, OFFS, CAP), I32),
        pltpu.VMEM((1, OFFS, CAP), I32),
        pltpu.VMEM((12, TILES, 8, 128), F32),
        pltpu.VMEM((OFFS, 304, F), F32),
        pltpu.VMEM((2, 608, 2048), BF16),
        pltpu.VMEM((2, 304, 1024), BF16),
        pltpu.VMEM((3, 592, 256), BF16),
        pltpu.VMEM((4, 1024), I32),
        pltpu.VMEM((1, 512), I32),
        pltpu.VMEM((2, 2048, 512), BF16),
        pltpu.VMEM((2, 2048, 256), BF16),
        pltpu.VMEM((2, 1024, 384), BF16),
        pltpu.VMEM((304, 256), F32),
        pltpu.VMEM((304, 128), F32),
        pltpu.VMEM((304, 128), F32),
        pltpu.VMEM((384, 256), BF16),
        pltpu.VMEM((256, 256), BF16),
        pltpu.VMEM((40, 128), F32),
        pltpu.VMEM((HALF, 256), F32),
        pltpu.VMEM((40, 128), F32),
        pltpu.VMEM((2, HALF, 128), F32),
        pltpu.VMEM((40, 128), F32),
        pltpu.VMEM((2, 120, 128), F32),
        pltpu.VMEM((HALF, 128), F32),
        pltpu.VMEM((40, 128), F32),
        pltpu.VMEM((2, 120, 128), F32),
        pltpu.VMEM((2, 120, 128), F32),
        pltpu.VMEM((2, HALF, 128), F32),
        pltpu.VMEM((2, HALF, 128), F32),
        pltpu.VMEM((2, 384, 128), F32),
        pltpu.VMEM((2, 128, 384), F32),
        pltpu.SemaphoreType.DMA((5,)),
        pltpu.SemaphoreType.DMA((OFFS,)),
        pltpu.SemaphoreType.DMA((5,)),
        pltpu.SemaphoreType.DMA((6,)),
        pltpu.SemaphoreType.DMA((12,)),
        pltpu.SemaphoreType.DMA((9,)),
        pltpu.SemaphoreType.DMA((9,)),
    ]
    return pl.pallas_call(
        kernel,
        out_shape=jax.ShapeDtypeStruct((ROWS, F), F32),
        in_specs=[pl.BlockSpec(memory_space=pltpu.HBM)] * 6,
        out_specs=vmem,
        scratch_shapes=scratch,
        compiler_params=pltpu.CompilerParams(
            collective_id=0, has_side_effects=True, vmem_limit_bytes=60 * 2**20
        ),
        name="translate",
    )(density, operators, owner_count[None], group_count[None], target_slot, source_box)


def solution(mesh):
    placed = (P(("box", "op"), None), P("op", None, None), P(), P(), P("box", "op", None), P("box", "op", None))
    return jax.shard_map(
        body, mesh=mesh, in_specs=placed, out_specs=P(("box", "op"), None), check_vma=False
    )
```

```python
import jax
import jax.numpy as jnp
from jax import lax
from jax.experimental import pallas as pl
from jax.experimental.pallas import tpu as pltpu
from jax.sharding import PartitionSpec as P

MESH = pl.DeviceIdType.MESH
F32, BF16, I32 = jnp.float32, jnp.bfloat16, jnp.int32
ROWS = 72
CAP = 288
EDGE = 96
F = 296
HALF = 152
STEP = 144
OFFS = 16
TILES = 21
SHORT = 15


def iota(shape, dim):
    return lax.broadcasted_iota(I32, shape, dim)


def split(v):
    hi = v.astype(BF16)
    lo = (v - hi.astype(F32)).astype(BF16)
    return hi, lo


def slot_of_column(col):
    main = 72 * (col >> 6) + (col & 63)
    c = col & 31
    left = 72 * (c >> 3) + 64 + (c & 7)
    return jnp.where(col < 256, main, left)


def start_at(counts, index):
    lane = iota(counts.shape, 1)
    return jnp.sum(jnp.where(lane < index, counts.astype(F32), 0.0), axis=1, keepdims=True).astype(I32)


def kernel(
    den_hbm, ops, ocnt_hbm, gcnt_hbm, tgt_hbm, src_hbm, out,
    den, ocnt, gcnt, tgt, src, rx, stage, o_main, o_left, xt, pmain, pleft, g_both, g_lo, g_last, acc, side, ufold,
    hot_send, hot_recv, lpack, ra, ral, q_ref, ql_ref, ht, rq, rql, hr, tr, qh, qt, v_ref, fr, fin, tt,
    in_sem, op_sem, ici_send, sib_send, rsem, osend, orecv,
):
    b, o = lax.axis_index("box"), lax.axis_index("op")
    n = lax.axis_size("box")
    core, chip = o % 2, o // 2
    far, sib = (o + 2) % 4, o + 1 - 2 * core
    up, down = (b + 1) % n, (b + n - 1) % n
    sibling, beside = (b, sib), (b, far)
    peers = [sibling, beside, (up, o), (up, far), (down, o), (down, far)]

    def op_copy(k):
        return pltpu.make_async_copy(ops.at[k], stage.at[k, pl.ds(0, F)], op_sem.at[k])

    barrier = pltpu.get_barrier_semaphore()
    for peer in peers:
        pl.semaphore_signal(barrier, inc=1, device_id=peer, device_id_type=MESH)
    pairs = ((den_hbm, den), (ocnt_hbm, ocnt), (gcnt_hbm, gcnt), (tgt_hbm, tgt), (src_hbm, src))
    inputs = [pltpu.make_async_copy(a, v, in_sem.at[i]) for i, (a, v) in enumerate(pairs)]
    for c in inputs:
        c.start()
    for k in range(OFFS):
        op_copy(k).start()
    inputs[0].wait()

    me = 4 + o
    for lt in range(3):
        parts = [den[8 * (lt + 3 * g) : 8 * (lt + 3 * g) + 8, 256:F] for g in range(3)]
        rx[me, lt] = jnp.concatenate([*parts, jnp.zeros((8, 8), F32)], axis=1)
    for rt in range(9):
        for h in range(2):
            rx[me, 3 + 2 * rt + h] = den[8 * rt : 8 * rt + 8, 128 * h : 128 * h + 128]

    for c in inputs[1:]:
        c.wait()
    counts_o, counts_g = ocnt[...], gcnt[...]
    os0, os1, os2 = (start_at(counts_o, b + i) for i in (-1, 0, 1))
    gs1, gs2 = (start_at(counts_g, b + i) for i in (0, 1))
    shift = gs1 - os1
    m = src[0]
    before, own = m - os0, m - os1
    before = 512 + jnp.where(before < 256, before, before - 256)
    own = jnp.where(own < 256, own, own + 192)
    place = jnp.where(m < os1, before, jnp.where(m < os2, own, 256 + m - os2))
    place = jnp.where(tgt[0] < CAP, place, -1)
    j = iota((CAP, 384), 0) + shift
    j = jnp.where(j < 0, j + CAP, jnp.where(j >= CAP, j - CAP, j))
    turn = jnp.where(j == slot_of_column(iota((CAP, 384), 1)), 1.0, 0.0).astype(F32)
    turned = jnp.dot(place.astype(F32), turn, precision=lax.Precision.HIGHEST, preferred_element_type=F32)
    turned = (turned + 0.25 * jnp.where(turned < 0, -1.0, 1.0)).astype(I32)
    lane_id = iota((1, 128), 1)
    group_of_lane = lane_id >> 5
    for i in range(4):
        pmain[i : i + 1] = jnp.concatenate([turned[k : k + 1, :256] for k in range(4 * i, 4 * i + 4)], axis=1)
        row = jnp.zeros((1, 128), I32)
        for a in range(4):
            row = jnp.where(group_of_lane == a, turned[4 * i + a : 4 * i + a + 1, 256:384], row)
        pleft[:, 128 * i : 128 * i + 128] = row

    s = slot_of_column(iota((256, 128), 0))
    lane = iota((256, 128), 1)
    is_head = (s >= CAP - EDGE) & (os1 + s - CAP >= gs1) & (s - (CAP - EDGE) == lane)
    box1 = os1 + s
    tail = jnp.where((box1 >= os2) & (box1 < gs2), box1 - os2, jnp.where(box1 + CAP < gs2, box1 + CAP - os2, -1))
    hot_send[:, :128] = jnp.where(is_head, 1.0, 0.0).astype(BF16)
    hot_send[:, 128:] = jnp.where(tail == lane, 1.0, 0.0).astype(BF16)
    r = iota((512, 128), 0)
    c = r & 127
    s = slot_of_column(256 + (c & 31))
    head = jnp.where((s >= CAP - EDGE) & (os2 + s - CAP >= gs2), os2 - os1 + s - CAP, -1)
    box0 = os0 + s
    tail = jnp.where((box0 >= os1) & (box0 < gs1), box0, jnp.where(box0 + CAP < gs1, box0 + CAP, -1))
    tail = jnp.where(tail >= 0, tail - os1, -1)
    far_slot = jnp.where(c < 32, jnp.where(r < 384, head, tail), -1)
    near_slot = jnp.where(c < EDGE, jnp.where(r < 128, os2 - os1 + c - EDGE, c), -1)
    slot = jnp.where(r < 256, near_slot, far_slot)
    lane = iota((512, 128), 1)
    hot_recv[:, :128] = jnp.where(slot == slot_of_column(lane + 128 * chip), 1.0, 0.0).astype(BF16)
    hot_recv[:, 128:] = jnp.where((lane < 32) & (slot == slot_of_column(lane + 256)), 1.0, 0.0).astype(BF16)

    def block_copy(here, there, count, send, device):
        return pltpu.make_async_remote_copy(
            src_ref=rx.at[here, pl.ds(0, count)], dst_ref=rx.at[there, pl.ds(0, count)],
            send_sem=send, recv_sem=rsem.at[there], device_id=device, device_id_type=MESH,
        )

    pl.semaphore_wait(barrier, len(peers))

    def to_prev_segment(i):
        return block_copy(me, o, TILES, ici_send.at[1 + i], peers[2 + i])

    def to_next_segment(i, count):
        return block_copy(me, 8 + o, count, ici_send.at[3 + i], peers[4 + i])

    to_beside = block_copy(me, me, TILES, ici_send.at[0], beside)
    to_sibling = block_copy(me, me, TILES, sib_send.at[0], sibling)
    for i in (1, 0):
        to_prev_segment(i).start()

        @pl.when(o < 2)
        def _():
            to_next_segment(i, TILES).start()

        @pl.when(o == 2)
        def _():
            to_next_segment(i, SHORT).start()

    to_beside.start()
    to_sibling.start()

    stage[:, pl.ds(F, 8), :] = jnp.zeros((OFFS, 8, F), F32)

    def split_eight(q, _):
        for a in range(8):
            k = 8 * q + a
            op_copy(k).wait()
            v = stage[k]
            hi = v.astype(BF16)
            hi32 = hi.astype(F32)
            lo32 = v - hi32
            o_main[q, :304, 256 * a : 256 * a + 256] = hi[:, :256]
            o_main[q, 304:, 256 * a : 256 * a + 256] = lo32[:, :256].astype(BF16)
            last = jnp.concatenate([hi32[:, 256:], hi32[:, 256:], lo32[:, 256:], jnp.zeros((304, 8), F32)], axis=1)
            o_left[q, :, 128 * a : 128 * a + 128] = last.astype(BF16)
        return 0

    def arrived(there, count=TILES):
        block_copy(there, there, count, ici_send.at[0], sibling).wait_recv()

    def hand_on(i, there, count=TILES):
        return block_copy(there, there, count, sib_send.at[i], sibling)

    def pass_own():
        arrived(4 + far)
        hand_on(1, 4 + far).start()

    def pass_prev():
        for i, there in ((2, o), (3, far)):
            arrived(there)
            hand_on(i, there).start()

    def pass_next():
        arrived(8 + core)
        hand_on(4, 8 + core).start()

        @pl.when(core == 0)
        def _():
            arrived(10, SHORT)
            hand_on(5, 10, SHORT).start()

    def row_tiles(segment, tiles):
        return [(4 * segment + r // 9, r % 9) for r in tiles]

    def wide_left(idx, rt):
        left = rx[idx, rt % 3]
        return rx[idx, 3 + 2 * rt], rx[idx, 4 + 2 * rt], pltpu.roll(left, 128 - 40 * (rt // 3), 1) if rt >= 3 else left

    def turn_rows(t, half, parts):
        cols = [jnp.concatenate(list(p), axis=0).T for p in zip(*parts)]
        v = jnp.concatenate([cols[0], cols[1], cols[2][:40]], axis=0)
        hi32 = v.astype(BF16).astype(F32)
        lo32 = v - hi32
        xt[t, :, 128 * half : 128 * half + 128] = jnp.concatenate(
            [hi32[:256], lo32[:256], hi32[256:F], lo32[256:F]], axis=0
        ).astype(BF16)

    def turn_own():
        for half in range(2):
            turn_rows(0, half, [wide_left(*a) for a in row_tiles(1, range(16 * half, 16 * half + 16))])

    def turn_next():
        turn_rows(1, 0, [wide_left(*a) for a in row_tiles(2, range(16))])
        parts = [wide_left(*a) for a in row_tiles(2, range(16, 24)) + row_tiles(1, range(32, 36))]
        turn_rows(1, 1, parts + [(jnp.zeros((8, 128), F32),) * 3] * 4)

    def turn_prev():
        parts = [wide_left(*a) for a in row_tiles(0, range(16))]
        folded = [wide_left(*a) for a in row_tiles(0, range(32, 36))]
        long = os1 - os0 > 256
        for r in range(4):
            parts[r] = tuple(jnp.where(long, x, y) for x, y in zip(folded[r], parts[r]))
        turn_rows(2, 0, parts)
        turn_rows(2, 1, [wide_left(*a) for a in row_tiles(0, range(16, 32))])

    def gathered(row, t):
        rows = xt[0] if t == 0 else jnp.concatenate([xt[1], xt[2]], axis=1)
        hot = jnp.where(iota((rows.shape[1], row.shape[1]), 0) + 256 * t == row, 1.0, 0.0).astype(BF16)
        return jnp.dot(rows, hot, preferred_element_type=F32)

    def put(q, a, g, left, add):
        tail = jnp.concatenate([g[512:592], g[512:552], jnp.zeros((8, g.shape[1]), F32)], axis=0)
        rows, short = pl.ds(256 * a, 256), pl.ds(128 * a, 128)
        for ref, at, columns, v in (
            (g_both, rows, pl.ds(256, 128) if left else pl.ds(0, 256), g[:256]),
            (g_both, rows, pl.ds(384, 128), g[256:512]) if left else (g_lo, rows, pl.ds(0, 256), g[256:512]),
            (g_last, short, pl.ds(256, 128) if left else pl.ds(0, 256), tail),
        ):
            v = v.astype(BF16)
            ref[q, at, columns] = ref[q, at, columns] + v if add else v

    def gather(t, add):
        def gather_eight(q, _):
            for h in range(2):
                g = gathered(pmain[pl.ds(2 * q + h, 1), :], t)
                for a in range(4):
                    put(q, 4 * h + a, g[:, 256 * a : 256 * a + 256], False, add)
            return 0

        lax.fori_loop(0, 2, gather_eight, 0)
        g = gathered(pleft[...], t)
        for k in range(OFFS):
            part = g[:, 128 * (k // 4) : 128 * (k // 4) + 128]
            put(k // 8, k % 8, jnp.where(group_of_lane == k % 4, part, 0.0), True, add)

    lax.fori_loop(0, 1, split_eight, 0)
    pass_own()
    lax.fori_loop(1, 2, split_eight, 0)
    even = b % 2 == 0
    pl.when(even)(pass_next)
    odd = jnp.logical_not(even)
    pl.when(odd)(pass_prev)

    pl.when(even)(pass_prev)
    pl.when(odd)(pass_next)
    arrived(4 + sib)
    arrived(4 + (sib + 2) % 4)
    turn_own()
    gather(0, False)
    for there in (sib, (sib + 2) % 4, 9 - core):
        arrived(there)

    @pl.when(core == 1)
    def _():
        arrived(10, SHORT)

    turn_next()
    turn_prev()
    gather(1, True)

    acc[...] = jnp.zeros(acc.shape, F32)
    side[...] = jnp.zeros(side.shape, F32)

    def multiply_main(q, _):
        both = jnp.dot(o_main[q], g_both[q, :, :256], preferred_element_type=F32)
        third = jnp.dot(o_main[q, :304], g_lo[q], preferred_element_type=F32)
        last = jnp.dot(o_left[q], g_last[q, :, :256], preferred_element_type=F32)
        acc[...] += both[:304] + both[304:] + third + last
        return 0

    def multiply_side(q, _):
        both = jnp.dot(o_main[q], g_both[q, :, 256:], preferred_element_type=F32)
        last = jnp.dot(o_left[q], g_last[q, :, 256:], preferred_element_type=F32)
        both = both[:304] + both[304:]
        side[...] += both[:, :128] + both[:, 128:] + last
        return 0

    lax.fori_loop(0, 2, multiply_main, 0)

    def packed(half):
        v = ufold[pl.ds(pl.multiple_of(STEP * half, 8), 160), :]
        row = jnp.zeros((40, 128), F32)
        for a in range(4):
            row = jnp.where(group_of_lane == a, v[40 * a : 40 * a + 40], row)
        return row

    def unpacked(v):
        parts = [v if a == 0 else pltpu.roll(v, 128 - 32 * a, 1) for a in range(4)]
        return jnp.concatenate(parts, axis=0)[:HALF]

    def send(i, source, target, device, recv=None):
        return pltpu.make_async_remote_copy(
            src_ref=source, dst_ref=target, send_sem=osend.at[i], recv_sem=orecv.at[i if recv is None else recv],
            device_id=device, device_id_type=MESH,
        )

    theirs = pl.ds(pl.multiple_of(STEP * (1 - core), 8), HALF)
    mine = pl.ds(pl.multiple_of(STEP * core, 8), HALF)
    swap = [send(0, acc.at[theirs], ra, sibling), send(1, lpack, ral, sibling)]
    swap[0].start()
    lax.fori_loop(0, 1, multiply_side, 0)
    swap[0].wait_recv()
    q0 = acc[mine, :128] + ra[:, :128]
    q1 = acc[mine, 128:256] + ra[:, 128:]
    q_ref[0], q_ref[1] = q0, q1
    hi, lo = split(jnp.concatenate([q0, q1], axis=1))
    edges = jnp.dot(hi, hot_send[...], preferred_element_type=F32)
    edges = edges + jnp.dot(lo, hot_send[...], preferred_element_type=F32)
    for i in range(2):
        e = jnp.concatenate([edges[:, 128 * i : 128 * i + 128], jnp.zeros((8, 128), F32)], axis=0)
        for a in range(3):
            ht[i, 40 * a : 40 * a + 40] = e[40 * a : 40 * a + 40] + jnp.where(
                lane_id >= EDGE, pltpu.roll(e[120:160], 96 - 32 * a, 1), 0.0
            )
    heads = [send(4 + i, ht.at[0], hr.at[chip], peers[4 + i], 4 + chip) for i in range(2)]
    tails = send(6, ht.at[1], tr.at[chip], (up, core), 6 + chip)
    cross = [send(2, q_ref.at[1 - chip], rq, beside), send(3, ql_ref, rql, beside)]
    for c in (heads[1], tails, heads[0], cross[0]):
        c.start()
    lax.fori_loop(1, 2, multiply_side, 0)
    u = side[...]
    u = u + pltpu.roll(u, 64, 1)
    ufold[...] = u + pltpu.roll(u, 32, 1)
    lpack[...] = packed(1 - core)
    swap[1].start()
    own_left = packed(core)
    swap[1].wait_recv()
    ql_ref[...] = own_left + ral[...]
    head_ql = [send(9 + i, ql_ref, qh.at[chip], peers[4 + i], 9 + chip) for i in range(2)]
    tail_ql = send(11, ql_ref, qt.at[chip], (up, core), 11 + chip)
    for c in (head_ql[1], tail_ql, head_ql[0], cross[1]):
        c.start()
    for c in cross:
        c.wait_recv()
    s = slot_of_column(iota((1, 128), 1) + 128 * chip)
    box1 = os1 + s
    keep = (box1 >= gs1) & (box1 < gs2) & (box1 < os2)
    own = jnp.where(keep, q_ref[chip] + rq[...], 0.0)
    box1 = os1 + slot_of_column(256 + (iota((1, 128), 1) & 31))
    keep = (box1 >= gs1) & (box1 < gs2) & (box1 < os2)
    own_left = unpacked(jnp.where(keep, ql_ref[...] + rql[...], 0.0))
    for i in range(2):
        send(4 + i, ht.at[0], hr.at[i], peers[4], 4 + i).wait_recv()
        send(9, ql_ref, qh.at[i], peers[4], 9 + i).wait_recv()

    @pl.when(chip == 0)
    def _():
        for i in range(2):
            send(6, ht.at[1], tr.at[i], peers[4], 6 + i).wait_recv()
            send(11, ql_ref, qt.at[i], peers[4], 11 + i).wait_recv()

    @pl.when(chip == 1)
    def _():
        tr[...] = jnp.zeros(tr.shape, F32)
        qt[...] = jnp.zeros(qt.shape, F32)

    def edge_rows(v):
        thirds = [pltpu.roll(v[40 * a : 40 * a + 40], 32 * a + 32, 1) for a in range(3)]
        quarter = jnp.where(lane_id < 32, thirds[0], jnp.where(lane_id < 64, thirds[1], thirds[2]))
        return jnp.concatenate([v, quarter], axis=0)[:HALF]

    near = [edge_rows(v[0] + v[1]) for v in (hr, tr)]
    hi, lo = split(jnp.concatenate([*near, unpacked(qh[0] + qh[1]), unpacked(qt[0] + qt[1])], axis=1))
    moved = jnp.dot(hi, hot_recv[...], preferred_element_type=F32) + jnp.dot(
        lo, hot_recv[...], preferred_element_type=F32
    )
    v0, v1 = own + moved[:, :128], own_left + moved[:, 128:]
    v_ref[0], v_ref[1] = v0, v1
    last = send(8, v_ref, fr, sibling)
    last.start()
    for i, v in enumerate((v0, v1)):
        fin[i, mine] = v
    last.wait_recv()
    for i in range(2):
        fin[i, theirs] = fr[i]
        tt[i] = fin[i].T
    out[0:64] = tt[0, pl.ds(pl.multiple_of(64 * core, 8), 64), :F]
    out[64:72] = tt[1, pl.ds(pl.multiple_of(8 * o, 8), 8), :F]

    for c in (to_beside, to_sibling, *(to_prev_segment(i) for i in range(2))):
        c.wait_send()
    for i, there in enumerate((4 + far, o, far, 8 + core)):
        hand_on(1 + i, there).wait_send()

    @pl.when(core == 0)
    def _():
        hand_on(5, 10, SHORT).wait_send()

    @pl.when(o < 2)
    def _():
        for i in range(2):
            to_next_segment(i, TILES).wait_send()

    @pl.when(o == 2)
    def _():
        for i in range(2):
            to_next_segment(i, SHORT).wait_send()

    for c in (*swap, *cross, *heads, tails, *head_ql, tail_ql, last):
        c.wait_send()


def body(density, operators, owner_count, group_count, target_slot, source_box):
    vmem = pl.BlockSpec(memory_space=pltpu.VMEM)
    scratch = [
        pltpu.VMEM((ROWS, F), F32),
        pltpu.VMEM(owner_count[None].shape, I32),
        pltpu.VMEM(group_count[None].shape, I32),
        pltpu.VMEM((1, OFFS, CAP), I32),
        pltpu.VMEM((1, OFFS, CAP), I32),
        pltpu.VMEM((12, TILES, 8, 128), F32),
        pltpu.VMEM((OFFS, 304, F), F32),
        pltpu.VMEM((2, 608, 2048), BF16),
        pltpu.VMEM((2, 304, 1024), BF16),
        pltpu.VMEM((3, 592, 256), BF16),
        pltpu.VMEM((4, 1024), I32),
        pltpu.VMEM((1, 512), I32),
        pltpu.VMEM((2, 2048, 512), BF16),
        pltpu.VMEM((2, 2048, 256), BF16),
        pltpu.VMEM((2, 1024, 384), BF16),
        pltpu.VMEM((304, 256), F32),
        pltpu.VMEM((304, 128), F32),
        pltpu.VMEM((304, 128), F32),
        pltpu.VMEM((256, 256), BF16),
        pltpu.VMEM((512, 256), BF16),
        pltpu.VMEM((40, 128), F32),
        pltpu.VMEM((HALF, 256), F32),
        pltpu.VMEM((40, 128), F32),
        pltpu.VMEM((2, HALF, 128), F32),
        pltpu.VMEM((40, 128), F32),
        pltpu.VMEM((2, 120, 128), F32),
        pltpu.VMEM((HALF, 128), F32),
        pltpu.VMEM((40, 128), F32),
        pltpu.VMEM((2, 120, 128), F32),
        pltpu.VMEM((2, 120, 128), F32),
        pltpu.VMEM((2, 40, 128), F32),
        pltpu.VMEM((2, 40, 128), F32),
        pltpu.VMEM((2, HALF, 128), F32),
        pltpu.VMEM((2, HALF, 128), F32),
        pltpu.VMEM((2, 384, 128), F32),
        pltpu.VMEM((2, 128, 384), F32),
        pltpu.SemaphoreType.DMA((5,)),
        pltpu.SemaphoreType.DMA((OFFS,)),
        pltpu.SemaphoreType.DMA((5,)),
        pltpu.SemaphoreType.DMA((6,)),
        pltpu.SemaphoreType.DMA((12,)),
        pltpu.SemaphoreType.DMA((12,)),
        pltpu.SemaphoreType.DMA((13,)),
    ]
    return pl.pallas_call(
        kernel,
        out_shape=jax.ShapeDtypeStruct((ROWS, F), F32),
        in_specs=[pl.BlockSpec(memory_space=pltpu.HBM)] * 6,
        out_specs=vmem,
        scratch_shapes=scratch,
        compiler_params=pltpu.CompilerParams(
            collective_id=0, has_side_effects=True, vmem_limit_bytes=60 * 2**20
        ),
        name="translate",
    )(density, operators, owner_count[None], group_count[None], target_slot, source_box)


def solution(mesh):
    placed = (P(("box", "op"), None), P("op", None, None), P(), P(), P("box", "op", None), P("box", "op", None))
    return jax.shard_map(
        body, mesh=mesh, in_specs=placed, out_specs=P(("box", "op"), None), check_vma=False
    )
```

```python
import jax
import jax.numpy as jnp
from jax import lax
from jax.experimental import pallas as pl
from jax.experimental.pallas import tpu as pltpu
from jax.sharding import PartitionSpec as P

MESH = pl.DeviceIdType.MESH
F32, BF16, I32 = jnp.float32, jnp.bfloat16, jnp.int32
ROWS = 72
CAP = 288
EDGE = 96
F = 296
HALF = 152
STEP = 144
OFFS = 16
TILES = 21
SHORT = 15


def iota(shape, dim):
    return lax.broadcasted_iota(I32, shape, dim)


def split(v):
    hi = v.astype(BF16)
    lo = (v - hi.astype(F32)).astype(BF16)
    return hi, lo


def slot_of_column(col):
    main = 72 * (col >> 6) + (col & 63)
    c = col & 31
    left = 72 * (c >> 3) + 64 + (c & 7)
    return jnp.where(col < 256, main, left)


def start_at(counts, index):
    lane = iota(counts.shape, 1)
    return jnp.sum(jnp.where(lane < index, counts.astype(F32), 0.0), axis=1, keepdims=True).astype(I32)


def kernel(
    den_hbm, ops, ocnt_hbm, gcnt_hbm, tgt_hbm, src_hbm, out,
    den, ocnt, gcnt, tgt, src, rx, stage, o_main, o_left, xt, pmain, pleft, g_both, g_lo, g_last, acc, side, ufold,
    hot_send, hot_recv, lpack, ra, ral, q_ref, ql_ref, ht, rq, rql, hr, tr, qh, qt, v_ref, fr, fin, tt,
    in_sem, op_sem, ici_send, sib_send, rsem, osend, orecv,
):
    b, o = lax.axis_index("box"), lax.axis_index("op")
    n = lax.axis_size("box")
    core, chip = o % 2, o // 2
    far, sib = (o + 2) % 4, o + 1 - 2 * core
    up, down = (b + 1) % n, (b + n - 1) % n
    sibling, beside = (b, sib), (b, far)
    peers = [sibling, beside, (up, o), (up, far), (down, o), (down, far)]
    has_down, has_up = b > 0, b < n - 1

    def op_copy(k):
        return pltpu.make_async_copy(ops.at[k], stage.at[k, pl.ds(0, F)], op_sem.at[k])

    barrier = pltpu.get_barrier_semaphore()


    def greet(some):
        for peer in some:
            pl.semaphore_signal(barrier, inc=1, device_id=peer, device_id_type=MESH)

    greet(peers[:2])
    pl.when(has_up)(lambda: greet(peers[2:4]))
    pl.when(has_down)(lambda: greet(peers[4:]))
    pairs = ((den_hbm, den), (ocnt_hbm, ocnt), (gcnt_hbm, gcnt), (tgt_hbm, tgt), (src_hbm, src))
    inputs = [pltpu.make_async_copy(a, v, in_sem.at[i]) for i, (a, v) in enumerate(pairs)]
    for c in inputs:
        c.start()
    for k in range(OFFS):
        op_copy(k).start()
    inputs[0].wait()

    me = 4 + o
    for lt in range(3):
        parts = [den[8 * (lt + 3 * g) : 8 * (lt + 3 * g) + 8, 256:F] for g in range(3)]
        rx[me, lt] = jnp.concatenate([*parts, jnp.zeros((8, 8), F32)], axis=1)
    for rt in range(9):
        for h in range(2):
            rx[me, 3 + 2 * rt + h] = den[8 * rt : 8 * rt + 8, 128 * h : 128 * h + 128]

    for c in inputs[1:]:
        c.wait()
    counts_o, counts_g = ocnt[...], gcnt[...]
    os0, os1, os2 = (start_at(counts_o, b + i) for i in (-1, 0, 1))
    gs1, gs2 = (start_at(counts_g, b + i) for i in (0, 1))
    shift = gs1 - os1
    m = src[0]
    before, own = m - os0, m - os1
    before = 512 + jnp.where(before < 256, before, before - 256)
    own = jnp.where(own < 256, own, own + 192)
    place = jnp.where(m < os1, before, jnp.where(m < os2, own, 256 + m - os2))
    place = jnp.where(tgt[0] < CAP, place, -1)
    j = iota((CAP, 384), 0) + shift
    j = jnp.where(j < 0, j + CAP, jnp.where(j >= CAP, j - CAP, j))
    turn = jnp.where(j == slot_of_column(iota((CAP, 384), 1)), 1.0, 0.0).astype(F32)
    turned = jnp.dot(place.astype(F32), turn, precision=lax.Precision.HIGHEST, preferred_element_type=F32)
    turned = (turned + 0.25 * jnp.where(turned < 0, -1.0, 1.0)).astype(I32)
    lane_id = iota((1, 128), 1)
    group_of_lane = lane_id >> 5
    for i in range(4):
        pmain[i : i + 1] = jnp.concatenate([turned[k : k + 1, :256] for k in range(4 * i, 4 * i + 4)], axis=1)
        row = jnp.zeros((1, 128), I32)
        for a in range(4):
            row = jnp.where(group_of_lane == a, turned[4 * i + a : 4 * i + a + 1, 256:384], row)
        pleft[:, 128 * i : 128 * i + 128] = row

    s = slot_of_column(iota((256, 128), 0))
    lane = iota((256, 128), 1)
    is_head = (s >= CAP - EDGE) & (os1 + s - CAP >= gs1) & (s - (CAP - EDGE) == lane)
    box1 = os1 + s
    tail = jnp.where((box1 >= os2) & (box1 < gs2), box1 - os2, jnp.where(box1 + CAP < gs2, box1 + CAP - os2, -1))
    hot_send[:, :128] = jnp.where(is_head, 1.0, 0.0).astype(BF16)
    hot_send[:, 128:] = jnp.where(tail == lane, 1.0, 0.0).astype(BF16)
    r = iota((512, 128), 0)
    c = r & 127
    s = slot_of_column(256 + (c & 31))
    head = jnp.where((s >= CAP - EDGE) & (os2 + s - CAP >= gs2), os2 - os1 + s - CAP, -1)
    box0 = os0 + s
    tail = jnp.where((box0 >= os1) & (box0 < gs1), box0, jnp.where(box0 + CAP < gs1, box0 + CAP, -1))
    tail = jnp.where(tail >= 0, tail - os1, -1)
    far_slot = jnp.where(c < 32, jnp.where(r < 384, head, tail), -1)
    near_slot = jnp.where(c < EDGE, jnp.where(r < 128, os2 - os1 + c - EDGE, c), -1)
    slot = jnp.where(r < 256, near_slot, far_slot)
    lane = iota((512, 128), 1)
    hot_recv[:, :128] = jnp.where(slot == slot_of_column(lane + 128 * chip), 1.0, 0.0).astype(BF16)
    hot_recv[:, 128:] = jnp.where((lane < 32) & (slot == slot_of_column(lane + 256)), 1.0, 0.0).astype(BF16)

    def block_copy(here, there, count, send, device):
        return pltpu.make_async_remote_copy(
            src_ref=rx.at[here, pl.ds(0, count)], dst_ref=rx.at[there, pl.ds(0, count)],
            send_sem=send, recv_sem=rsem.at[there], device_id=device, device_id_type=MESH,
        )

    pl.semaphore_wait(barrier, jnp.where(has_up & has_down, 6, 4))

    def to_prev_segment(i):
        return block_copy(me, o, TILES, ici_send.at[1 + i], peers[2 + i])

    def to_next_segment(i, count):
        return block_copy(me, 8 + o, count, ici_send.at[3 + i], peers[4 + i])

    to_beside = block_copy(me, me, TILES, ici_send.at[0], beside)
    to_sibling = block_copy(me, me, TILES, sib_send.at[0], sibling)
    for i in (1, 0):

        @pl.when(has_up)
        def _():
            to_prev_segment(i).start()

        @pl.when(has_down & (o < 2))
        def _():
            to_next_segment(i, TILES).start()

        @pl.when(has_down & (o == 2))
        def _():
            to_next_segment(i, SHORT).start()

    to_beside.start()
    to_sibling.start()

    stage[:, pl.ds(F, 8), :] = jnp.zeros((OFFS, 8, F), F32)

    def split_eight(q, _):
        for a in range(8):
            k = 8 * q + a
            op_copy(k).wait()
            v = stage[k]
            hi = v.astype(BF16)
            hi32 = hi.astype(F32)
            lo32 = v - hi32
            o_main[q, :304, 256 * a : 256 * a + 256] = hi[:, :256]
            o_main[q, 304:, 256 * a : 256 * a + 256] = lo32[:, :256].astype(BF16)
            last = jnp.concatenate([hi32[:, 256:], hi32[:, 256:], lo32[:, 256:], jnp.zeros((304, 8), F32)], axis=1)
            o_left[q, :, 128 * a : 128 * a + 128] = last.astype(BF16)
        return 0

    def arrived(there, count=TILES):
        block_copy(there, there, count, ici_send.at[0], sibling).wait_recv()

    def hand_on(i, there, count=TILES):
        return block_copy(there, there, count, sib_send.at[i], sibling)

    def pass_own():
        arrived(4 + far)
        hand_on(1, 4 + far).start()

    def pass_prev():
        for i, there in ((2, o), (3, far)):
            arrived(there)
            hand_on(i, there).start()

    def pass_next():
        arrived(8 + core)
        hand_on(4, 8 + core).start()

        @pl.when(core == 0)
        def _():
            arrived(10, SHORT)
            hand_on(5, 10, SHORT).start()

    def row_tiles(segment, tiles):
        return [(4 * segment + r // 9, r % 9) for r in tiles]

    def wide_left(idx, rt):
        left = rx[idx, rt % 3]
        return rx[idx, 3 + 2 * rt], rx[idx, 4 + 2 * rt], pltpu.roll(left, 128 - 40 * (rt // 3), 1) if rt >= 3 else left

    def turn_rows(t, half, parts):
        cols = [jnp.concatenate(list(p), axis=0).T for p in zip(*parts)]
        v = jnp.concatenate([cols[0], cols[1], cols[2][:40]], axis=0)
        hi32 = v.astype(BF16).astype(F32)
        lo32 = v - hi32
        xt[t, :, 128 * half : 128 * half + 128] = jnp.concatenate(
            [hi32[:256], lo32[:256], hi32[256:F], lo32[256:F]], axis=0
        ).astype(BF16)

    def turn_own():
        for half in range(2):
            turn_rows(0, half, [wide_left(*a) for a in row_tiles(1, range(16 * half, 16 * half + 16))])

    def turn_next():
        turn_rows(1, 0, [wide_left(*a) for a in row_tiles(2, range(16))])
        parts = [wide_left(*a) for a in row_tiles(2, range(16, 24)) + row_tiles(1, range(32, 36))]
        turn_rows(1, 1, parts + [(jnp.zeros((8, 128), F32),) * 3] * 4)

    def turn_prev():
        parts = [wide_left(*a) for a in row_tiles(0, range(16))]
        folded = [wide_left(*a) for a in row_tiles(0, range(32, 36))]
        long = os1 - os0 > 256
        for r in range(4):
            parts[r] = tuple(jnp.where(long, x, y) for x, y in zip(folded[r], parts[r]))
        turn_rows(2, 0, parts)
        turn_rows(2, 1, [wide_left(*a) for a in row_tiles(0, range(16, 32))])

    def gathered(row, t):
        rows = xt[0] if t == 0 else jnp.concatenate([xt[1], xt[2]], axis=1)
        hot = jnp.where(iota((rows.shape[1], row.shape[1]), 0) + 256 * t == row, 1.0, 0.0).astype(BF16)
        return jnp.dot(rows, hot, preferred_element_type=F32)

    def put(q, a, g, left, add):
        tail = jnp.concatenate([g[512:592], g[512:552], jnp.zeros((8, g.shape[1]), F32)], axis=0)
        rows, short = pl.ds(256 * a, 256), pl.ds(128 * a, 128)
        for ref, at, columns, v in (
            (g_both, rows, pl.ds(256, 128) if left else pl.ds(0, 256), g[:256]),
            (g_both, rows, pl.ds(384, 128), g[256:512]) if left else (g_lo, rows, pl.ds(0, 256), g[256:512]),
            (g_last, short, pl.ds(256, 128) if left else pl.ds(0, 256), tail),
        ):
            v = v.astype(BF16)
            ref[q, at, columns] = ref[q, at, columns] + v if add else v

    def gather_main(t, add):
        def gather_eight(q, _):
            for h in range(2):
                g = gathered(pmain[pl.ds(2 * q + h, 1), :], t)
                for a in range(4):
                    put(q, 4 * h + a, g[:, 256 * a : 256 * a + 256], False, add)
            return 0

        lax.fori_loop(0, 2, gather_eight, 0)

    def gather_left(t, add):
        g = gathered(pleft[...], t)
        for k in range(OFFS):
            part = g[:, 128 * (k // 4) : 128 * (k // 4) + 128]
            put(k // 8, k % 8, jnp.where(group_of_lane == k % 4, part, 0.0), True, add)

    @pl.when(jnp.logical_not(has_down))
    def _():
        rx[0:4] = jnp.zeros((4, TILES, 8, 128), F32)

    @pl.when(jnp.logical_not(has_up))
    def _():
        rx[8:11] = jnp.zeros((3, TILES, 8, 128), F32)

    lax.fori_loop(0, 1, split_eight, 0)
    pass_own()
    lax.fori_loop(1, 2, split_eight, 0)
    even = b % 2 == 0
    odd = jnp.logical_not(even)
    pl.when(even & has_up)(pass_next)
    pl.when(odd & has_down)(pass_prev)
    pl.when(even & has_down)(pass_prev)
    pl.when(odd & has_up)(pass_next)
    arrived(4 + sib)
    arrived(4 + (sib + 2) % 4)
    turn_own()
    gather_main(0, False)
    gather_left(0, False)

    @pl.when(has_down)
    def _():
        arrived(sib)
        arrived((sib + 2) % 4)

    @pl.when(has_up)
    def _():
        arrived(9 - core)

    @pl.when(has_up & (core == 1))
    def _():
        arrived(10, SHORT)

    turn_next()
    turn_prev()
    gather_main(1, True)

    acc[...] = jnp.zeros(acc.shape, F32)
    side[...] = jnp.zeros(side.shape, F32)

    def multiply_main(q, _):
        both = jnp.dot(o_main[q], g_both[q, :, :256], preferred_element_type=F32)
        third = jnp.dot(o_main[q, :304], g_lo[q], preferred_element_type=F32)
        last = jnp.dot(o_left[q], g_last[q, :, :256], preferred_element_type=F32)
        acc[...] += both[:304] + both[304:] + third + last
        return 0

    def multiply_side(q, _):
        both = jnp.dot(o_main[q], g_both[q, :, 256:], preferred_element_type=F32)
        last = jnp.dot(o_left[q], g_last[q, :, 256:], preferred_element_type=F32)
        both = both[:304] + both[304:]
        side[...] += both[:, :128] + both[:, 128:] + last
        return 0

    lax.fori_loop(0, 2, multiply_main, 0)

    def packed(half):
        v = ufold[pl.ds(pl.multiple_of(STEP * half, 8), 160), :]
        row = jnp.zeros((40, 128), F32)
        for a in range(4):
            row = jnp.where(group_of_lane == a, v[40 * a : 40 * a + 40], row)
        return row

    def unpacked(v):
        parts = [v if a == 0 else pltpu.roll(v, 128 - 32 * a, 1) for a in range(4)]
        return jnp.concatenate(parts, axis=0)[:HALF]

    def send(i, source, target, device, recv=None):
        return pltpu.make_async_remote_copy(
            src_ref=source, dst_ref=target, send_sem=osend.at[i], recv_sem=orecv.at[i if recv is None else recv],
            device_id=device, device_id_type=MESH,
        )

    theirs = pl.ds(pl.multiple_of(STEP * (1 - core), 8), HALF)
    mine = pl.ds(pl.multiple_of(STEP * core, 8), HALF)
    swap = [send(0, acc.at[theirs], ra, sibling), send(1, lpack, ral, sibling)]
    swap[0].start()
    gather_left(1, True)
    swap[0].wait_recv()
    q0 = acc[mine, :128] + ra[:, :128]
    q1 = acc[mine, 128:256] + ra[:, 128:]
    q_ref[0], q_ref[1] = q0, q1
    hi, lo = split(jnp.concatenate([q0, q1], axis=1))
    edges = jnp.dot(hi, hot_send[...], preferred_element_type=F32)
    edges = edges + jnp.dot(lo, hot_send[...], preferred_element_type=F32)
    for i in range(2):
        e = jnp.concatenate([edges[:, 128 * i : 128 * i + 128], jnp.zeros((8, 128), F32)], axis=0)
        for a in range(3):
            ht[i, 40 * a : 40 * a + 40] = e[40 * a : 40 * a + 40] + jnp.where(
                lane_id >= EDGE, pltpu.roll(e[120:160], 96 - 32 * a, 1), 0.0
            )
    heads = [send(4 + i, ht.at[0], hr.at[chip], peers[4 + i], 4 + chip) for i in range(2)]
    tails = send(6, ht.at[1], tr.at[chip], (up, core), 6 + chip)
    cross = [send(2, q_ref.at[1 - chip], rq, beside), send(3, ql_ref, rql, beside)]

    def with_up(name, *copies):
        for c in copies:
            pl.when(has_up)(c.start if name == "start" else c.wait_send)

    def with_down(name, *copies):
        for c in copies:
            pl.when(has_down)(c.start if name == "start" else c.wait_send)

    with_down("start", heads[1])
    with_up("start", tails)
    with_down("start", heads[0])
    cross[0].start()
    lax.fori_loop(0, 2, multiply_side, 0)
    u = side[...]
    u = u + pltpu.roll(u, 64, 1)
    ufold[...] = u + pltpu.roll(u, 32, 1)
    lpack[...] = packed(1 - core)
    swap[1].start()
    own_left = packed(core)
    swap[1].wait_recv()
    ql_ref[...] = own_left + ral[...]
    head_ql = [send(9 + i, ql_ref, qh.at[chip], peers[4 + i], 9 + chip) for i in range(2)]
    tail_ql = send(11, ql_ref, qt.at[chip], (up, core), 11 + chip)
    with_down("start", head_ql[1])
    with_up("start", tail_ql)
    with_down("start", head_ql[0])
    cross[1].start()
    for c in cross:
        c.wait_recv()
    s = slot_of_column(iota((1, 128), 1) + 128 * chip)
    box1 = os1 + s
    keep = (box1 >= gs1) & (box1 < gs2) & (box1 < os2)
    own = jnp.where(keep, q_ref[chip] + rq[...], 0.0)
    box1 = os1 + slot_of_column(256 + (iota((1, 128), 1) & 31))
    keep = (box1 >= gs1) & (box1 < gs2) & (box1 < os2)
    own_left = unpacked(jnp.where(keep, ql_ref[...] + rql[...], 0.0))
    @pl.when(has_up)
    def _():
        for i in range(2):
            send(4 + i, ht.at[0], hr.at[i], peers[4], 4 + i).wait_recv()
            send(9, ql_ref, qh.at[i], peers[4], 9 + i).wait_recv()

    @pl.when(jnp.logical_not(has_up))
    def _():
        hr[...] = jnp.zeros(hr.shape, F32)
        qh[...] = jnp.zeros(qh.shape, F32)

    takes_tails = has_down & (chip == 0)

    @pl.when(takes_tails)
    def _():
        for i in range(2):
            send(6, ht.at[1], tr.at[i], peers[4], 6 + i).wait_recv()
            send(11, ql_ref, qt.at[i], peers[4], 11 + i).wait_recv()

    @pl.when(jnp.logical_not(takes_tails))
    def _():
        tr[...] = jnp.zeros(tr.shape, F32)
        qt[...] = jnp.zeros(qt.shape, F32)

    def edge_rows(v):
        thirds = [pltpu.roll(v[40 * a : 40 * a + 40], 32 * a + 32, 1) for a in range(3)]
        quarter = jnp.where(lane_id < 32, thirds[0], jnp.where(lane_id < 64, thirds[1], thirds[2]))
        return jnp.concatenate([v, quarter], axis=0)[:HALF]

    near = [edge_rows(v[0] + v[1]) for v in (hr, tr)]
    hi, lo = split(jnp.concatenate([*near, unpacked(qh[0] + qh[1]), unpacked(qt[0] + qt[1])], axis=1))
    moved = jnp.dot(hi, hot_recv[...], preferred_element_type=F32) + jnp.dot(
        lo, hot_recv[...], preferred_element_type=F32
    )
    v0, v1 = own + moved[:, :128], own_left + moved[:, 128:]
    v_ref[0], v_ref[1] = v0, v1
    last = send(8, v_ref, fr, sibling)
    last.start()
    for i, v in enumerate((v0, v1)):
        fin[i, mine] = v
    last.wait_recv()
    for i in range(2):
        fin[i, theirs] = fr[i]
        tt[i] = fin[i].T
    out[0:64] = tt[0, pl.ds(pl.multiple_of(64 * core, 8), 64), :F]
    out[64:72] = tt[1, pl.ds(pl.multiple_of(8 * o, 8), 8), :F]

    for c in (to_beside, to_sibling, hand_on(1, 4 + far), *swap, *cross, last):
        c.wait_send()
    with_up("wait_send", to_prev_segment(0), to_prev_segment(1), hand_on(4, 8 + core), tails, tail_ql)
    with_down("wait_send", hand_on(2, o), hand_on(3, far), *heads, *head_ql)

    @pl.when(has_up & (core == 0))
    def _():
        hand_on(5, 10, SHORT).wait_send()

    @pl.when(has_down & (o < 2))
    def _():
        for i in range(2):
            to_next_segment(i, TILES).wait_send()

    @pl.when(has_down & (o == 2))
    def _():
        for i in range(2):
            to_next_segment(i, SHORT).wait_send()


def body(density, operators, owner_count, group_count, target_slot, source_box):
    vmem = pl.BlockSpec(memory_space=pltpu.VMEM)
    scratch = [
        pltpu.VMEM((ROWS, F), F32),
        pltpu.VMEM(owner_count[None].shape, I32),
        pltpu.VMEM(group_count[None].shape, I32),
        pltpu.VMEM((1, OFFS, CAP), I32),
        pltpu.VMEM((1, OFFS, CAP), I32),
        pltpu.VMEM((12, TILES, 8, 128), F32),
        pltpu.VMEM((OFFS, 304, F), F32),
        pltpu.VMEM((2, 608, 2048), BF16),
        pltpu.VMEM((2, 304, 1024), BF16),
        pltpu.VMEM((3, 592, 256), BF16),
        pltpu.VMEM((4, 1024), I32),
        pltpu.VMEM((1, 512), I32),
        pltpu.VMEM((2, 2048, 512), BF16),
        pltpu.VMEM((2, 2048, 256), BF16),
        pltpu.VMEM((2, 1024, 384), BF16),
        pltpu.VMEM((304, 256), F32),
        pltpu.VMEM((304, 128), F32),
        pltpu.VMEM((304, 128), F32),
        pltpu.VMEM((256, 256), BF16),
        pltpu.VMEM((512, 256), BF16),
        pltpu.VMEM((40, 128), F32),
        pltpu.VMEM((HALF, 256), F32),
        pltpu.VMEM((40, 128), F32),
        pltpu.VMEM((2, HALF, 128), F32),
        pltpu.VMEM((40, 128), F32),
        pltpu.VMEM((2, 120, 128), F32),
        pltpu.VMEM((HALF, 128), F32),
        pltpu.VMEM((40, 128), F32),
        pltpu.VMEM((2, 120, 128), F32),
        pltpu.VMEM((2, 120, 128), F32),
        pltpu.VMEM((2, 40, 128), F32),
        pltpu.VMEM((2, 40, 128), F32),
        pltpu.VMEM((2, HALF, 128), F32),
        pltpu.VMEM((2, HALF, 128), F32),
        pltpu.VMEM((2, 384, 128), F32),
        pltpu.VMEM((2, 128, 384), F32),
        pltpu.SemaphoreType.DMA((5,)),
        pltpu.SemaphoreType.DMA((OFFS,)),
        pltpu.SemaphoreType.DMA((5,)),
        pltpu.SemaphoreType.DMA((6,)),
        pltpu.SemaphoreType.DMA((12,)),
        pltpu.SemaphoreType.DMA((12,)),
        pltpu.SemaphoreType.DMA((13,)),
    ]
    return pl.pallas_call(
        kernel,
        out_shape=jax.ShapeDtypeStruct((ROWS, F), F32),
        in_specs=[pl.BlockSpec(memory_space=pltpu.HBM)] * 6,
        out_specs=vmem,
        scratch_shapes=scratch,
        compiler_params=pltpu.CompilerParams(
            collective_id=0, has_side_effects=True, vmem_limit_bytes=60 * 2**20
        ),
        name="translate",
    )(density, operators, owner_count[None], group_count[None], target_slot, source_box)


def solution(mesh):
    placed = (P(("box", "op"), None), P("op", None, None), P(), P(), P("box", "op", None), P("box", "op", None))
    return jax.shard_map(
        body, mesh=mesh, in_specs=placed, out_specs=P(("box", "op"), None), check_vma=False
    )
```

```python
import jax
import jax.numpy as jnp
from jax import lax
from jax.experimental import pallas as pl
from jax.experimental.pallas import tpu as pltpu
from jax.sharding import PartitionSpec as P

MESH = pl.DeviceIdType.MESH
F32, BF16, I32 = jnp.float32, jnp.bfloat16, jnp.int32
ROWS = 72
CAP = 288
EDGE = 96
F = 296
HALF = 152
STEP = 144
OFFS = 16
TILES = 21
SHORT = 15


def iota(shape, dim):
    return lax.broadcasted_iota(I32, shape, dim)


def split(v):
    hi = v.astype(BF16)
    lo = (v - hi.astype(F32)).astype(BF16)
    return hi, lo


def slot_of_column(col):
    main = 72 * (col >> 6) + (col & 63)
    c = col & 31
    left = 72 * (c >> 3) + 64 + (c & 7)
    return jnp.where(col < 256, main, left)


def start_at(counts, index):
    lane = iota(counts.shape, 1)
    return jnp.sum(jnp.where(lane < index, counts.astype(F32), 0.0), axis=1, keepdims=True).astype(I32)


def kernel(
    den_hbm, ops, ocnt_hbm, gcnt_hbm, tgt_hbm, src_hbm, out,
    den, ocnt, gcnt, tgt, src, rx, stage, o_main, o_left, xt, pmain, pleft, g_both, g_lo, g_last, acc, side, ufold,
    hot_send, hot_recv, lpack, ra, ral, q_ref, ql_ref, ht, rq, rql, hr, tr, qh, qt, v_ref, fr, fin, tt,
    in_sem, op_sem, ici_send, sib_send, rsem, osend, orecv,
):
    b, o = lax.axis_index("box"), lax.axis_index("op")
    n = lax.axis_size("box")
    core, chip = o % 2, o // 2
    far, sib = (o + 2) % 4, o + 1 - 2 * core
    up, down = (b + 1) % n, (b + n - 1) % n
    sibling, beside = (b, sib), (b, far)
    peers = [sibling, beside, (up, o), (up, far), (down, o), (down, far)]
    has_down, has_up = b > 0, b < n - 1

    def op_copy(k):
        return pltpu.make_async_copy(ops.at[k], stage.at[k, pl.ds(0, F)], op_sem.at[k])

    barrier = pltpu.get_barrier_semaphore()


    def greet(some):
        for peer in some:
            pl.semaphore_signal(barrier, inc=1, device_id=peer, device_id_type=MESH)

    greet(peers[:2])
    pl.when(has_up)(lambda: greet(peers[2:4]))
    pl.when(has_down)(lambda: greet(peers[4:]))
    pairs = ((den_hbm, den), (ocnt_hbm, ocnt), (gcnt_hbm, gcnt), (tgt_hbm, tgt), (src_hbm, src))
    inputs = [pltpu.make_async_copy(a, v, in_sem.at[i]) for i, (a, v) in enumerate(pairs)]
    for c in inputs:
        c.start()
    for k in range(OFFS):
        op_copy(k).start()
    inputs[0].wait()

    me = 4 + o
    for lt in range(3):
        parts = [den[8 * (lt + 3 * g) : 8 * (lt + 3 * g) + 8, 256:F] for g in range(3)]
        rx[me, lt] = jnp.concatenate([*parts, jnp.zeros((8, 8), F32)], axis=1)
    for rt in range(9):
        for h in range(2):
            rx[me, 3 + 2 * rt + h] = den[8 * rt : 8 * rt + 8, 128 * h : 128 * h + 128]

    for c in inputs[1:]:
        c.wait()
    counts_o, counts_g = ocnt[...], gcnt[...]
    os0, os1, os2 = (start_at(counts_o, b + i) for i in (-1, 0, 1))
    gs1, gs2 = (start_at(counts_g, b + i) for i in (0, 1))
    shift = gs1 - os1
    m = src[0]
    before, own = m - os0, m - os1
    before = 512 + jnp.where(before < 256, before, before - 256)
    own = jnp.where(own < 256, own, own + 192)
    place = jnp.where(m < os1, before, jnp.where(m < os2, own, 256 + m - os2))
    place = jnp.where(tgt[0] < CAP, place, -1)
    j = iota((CAP, 384), 0) + shift
    j = jnp.where(j < 0, j + CAP, jnp.where(j >= CAP, j - CAP, j))
    turn = jnp.where(j == slot_of_column(iota((CAP, 384), 1)), 1.0, 0.0).astype(F32)
    turned = jnp.dot(place.astype(F32), turn, precision=lax.Precision.HIGHEST, preferred_element_type=F32)
    turned = (turned + 0.25 * jnp.where(turned < 0, -1.0, 1.0)).astype(I32)
    lane_id = iota((1, 128), 1)
    group_of_lane = lane_id >> 5
    for i in range(4):
        pmain[i : i + 1] = jnp.concatenate([turned[k : k + 1, :256] for k in range(4 * i, 4 * i + 4)], axis=1)
        row = jnp.zeros((1, 128), I32)
        for a in range(4):
            row = jnp.where(group_of_lane == a, turned[4 * i + a : 4 * i + a + 1, 256:384], row)
        pleft[:, 128 * i : 128 * i + 128] = row

    s = slot_of_column(iota((256, 128), 0))
    lane = iota((256, 128), 1)
    is_head = (s >= CAP - EDGE) & (os1 + s - CAP >= gs1) & (s - (CAP - EDGE) == lane)
    box1 = os1 + s
    tail = jnp.where((box1 >= os2) & (box1 < gs2), box1 - os2, jnp.where(box1 + CAP < gs2, box1 + CAP - os2, -1))
    hot_send[:, :128] = jnp.where(is_head, 1.0, 0.0).astype(BF16)
    hot_send[:, 128:] = jnp.where(tail == lane, 1.0, 0.0).astype(BF16)
    r = iota((512, 128), 0)
    c = r & 127
    s = slot_of_column(256 + (c & 31))
    head = jnp.where((s >= CAP - EDGE) & (os2 + s - CAP >= gs2), os2 - os1 + s - CAP, -1)
    box0 = os0 + s
    tail = jnp.where((box0 >= os1) & (box0 < gs1), box0, jnp.where(box0 + CAP < gs1, box0 + CAP, -1))
    tail = jnp.where(tail >= 0, tail - os1, -1)
    far_slot = jnp.where(c < 32, jnp.where(r < 384, head, tail), -1)
    near_slot = jnp.where(c < EDGE, jnp.where(r < 128, os2 - os1 + c - EDGE, c), -1)
    slot = jnp.where(r < 256, near_slot, far_slot)
    lane = iota((512, 128), 1)
    hot_recv[:, :128] = jnp.where(slot == slot_of_column(lane + 128 * chip), 1.0, 0.0).astype(BF16)
    hot_recv[:, 128:] = jnp.where((lane < 32) & (slot == slot_of_column(lane + 256)), 1.0, 0.0).astype(BF16)

    def block_copy(here, there, count, send, device):
        return pltpu.make_async_remote_copy(
            src_ref=rx.at[here, pl.ds(0, count)], dst_ref=rx.at[there, pl.ds(0, count)],
            send_sem=send, recv_sem=rsem.at[there], device_id=device, device_id_type=MESH,
        )

    pl.semaphore_wait(barrier, jnp.where(has_up & has_down, 6, 4))

    def to_prev_segment(i):
        return block_copy(me, o, TILES, ici_send.at[1 + i], peers[2 + i])

    def to_next_segment(i, count):
        return block_copy(me, 8 + o, count, ici_send.at[3 + i], peers[4 + i])

    to_beside = block_copy(me, me, TILES, ici_send.at[0], beside)
    to_sibling = block_copy(me, me, TILES, sib_send.at[0], sibling)
    for i in (1, 0):

        @pl.when(has_up)
        def _():
            to_prev_segment(i).start()

        @pl.when(has_down & (o < 2))
        def _():
            to_next_segment(i, TILES).start()

        @pl.when(has_down & (o == 2))
        def _():
            to_next_segment(i, SHORT).start()

    to_beside.start()
    to_sibling.start()

    stage[:, pl.ds(F, 8), :] = jnp.zeros((OFFS, 8, F), F32)

    def split_eight(q, _):
        for a in range(8):
            k = 8 * q + a
            op_copy(k).wait()
            v = stage[k]
            hi = v.astype(BF16)
            hi32 = hi.astype(F32)
            lo32 = v - hi32
            o_main[q, :304, 256 * a : 256 * a + 256] = hi[:, :256]
            o_main[q, 304:, 256 * a : 256 * a + 256] = lo32[:, :256].astype(BF16)
            last = jnp.concatenate([hi32[:, 256:], hi32[:, 256:], lo32[:, 256:], jnp.zeros((304, 8), F32)], axis=1)
            o_left[q, :, 128 * a : 128 * a + 128] = last.astype(BF16)
        return 0

    def arrived(there, count=TILES):
        block_copy(there, there, count, ici_send.at[0], sibling).wait_recv()

    def hand_on(i, there, count=TILES):
        return block_copy(there, there, count, sib_send.at[i], sibling)

    def pass_own():
        arrived(4 + far)
        hand_on(1, 4 + far).start()

    def pass_prev():
        for i, there in ((2, o), (3, far)):
            arrived(there)
            hand_on(i, there).start()

    def pass_next():
        arrived(8 + core)
        hand_on(4, 8 + core).start()

        @pl.when(core == 0)
        def _():
            arrived(10, SHORT)
            hand_on(5, 10, SHORT).start()

    def row_tiles(segment, tiles):
        return [(4 * segment + r // 9, r % 9) for r in tiles]

    def wide_left(idx, rt):
        left = rx[idx, rt % 3]
        return rx[idx, 3 + 2 * rt], rx[idx, 4 + 2 * rt], pltpu.roll(left, 128 - 40 * (rt // 3), 1) if rt >= 3 else left

    def turn_rows(t, half, parts):
        cols = [jnp.concatenate(list(p), axis=0).T for p in zip(*parts)]
        v = jnp.concatenate([cols[0], cols[1], cols[2][:40]], axis=0)
        hi32 = v.astype(BF16).astype(F32)
        lo32 = v - hi32
        xt[t, :, 128 * half : 128 * half + 128] = jnp.concatenate(
            [hi32[:256], lo32[:256], hi32[256:F], lo32[256:F]], axis=0
        ).astype(BF16)

    def turn_own():
        for half in range(2):
            turn_rows(0, half, [wide_left(*a) for a in row_tiles(1, range(16 * half, 16 * half + 16))])

    def turn_next():
        turn_rows(1, 0, [wide_left(*a) for a in row_tiles(2, range(16))])
        parts = [wide_left(*a) for a in row_tiles(2, range(16, 24)) + row_tiles(1, range(32, 36))]
        turn_rows(1, 1, parts + [(jnp.zeros((8, 128), F32),) * 3] * 4)

    def turn_prev():
        parts = [wide_left(*a) for a in row_tiles(0, range(16))]
        folded = [wide_left(*a) for a in row_tiles(0, range(32, 36))]
        long = os1 - os0 > 256
        for r in range(4):
            parts[r] = tuple(jnp.where(long, x, y) for x, y in zip(folded[r], parts[r]))
        turn_rows(2, 0, parts)
        turn_rows(2, 1, [wide_left(*a) for a in row_tiles(0, range(16, 32))])

    def gathered(row, t):
        rows = xt[0] if t == 0 else jnp.concatenate([xt[1], xt[2]], axis=1)
        hot = jnp.where(iota((rows.shape[1], row.shape[1]), 0) + 256 * t == row, 1.0, 0.0).astype(BF16)
        return jnp.dot(rows, hot, preferred_element_type=F32)

    def put(q, a, g, left, add):
        tail = jnp.concatenate([g[512:592], g[512:552], jnp.zeros((8, g.shape[1]), F32)], axis=0)
        rows, short = pl.ds(256 * a, 256), pl.ds(128 * a, 128)
        for ref, at, columns, v in (
            (g_both, rows, pl.ds(256, 128) if left else pl.ds(0, 256), g[:256]),
            (g_both, rows, pl.ds(384, 128), g[256:512]) if left else (g_lo, rows, pl.ds(0, 256), g[256:512]),
            (g_last, short, pl.ds(256, 128) if left else pl.ds(0, 256), tail),
        ):
            v = v.astype(BF16)
            ref[q, at, columns] = ref[q, at, columns] + v if add else v

    def gather_main(t, add):
        def gather_eight(q, _):
            for h in range(2):
                g = gathered(pmain[pl.ds(2 * q + h, 1), :], t)
                for a in range(4):
                    put(q, 4 * h + a, g[:, 256 * a : 256 * a + 256], False, add)
            return 0

        lax.fori_loop(0, 2, gather_eight, 0)

    def gather_left(t, add):
        g = gathered(pleft[...], t)
        for k in range(OFFS):
            part = g[:, 128 * (k // 4) : 128 * (k // 4) + 128]
            put(k // 8, k % 8, jnp.where(group_of_lane == k % 4, part, 0.0), True, add)

    @pl.when(jnp.logical_not(has_down))
    def _():
        rx[0:4] = jnp.zeros((4, TILES, 8, 128), F32)

    @pl.when(jnp.logical_not(has_up))
    def _():
        rx[8:11] = jnp.zeros((3, TILES, 8, 128), F32)

    lax.fori_loop(0, 1, split_eight, 0)
    pass_own()
    lax.fori_loop(1, 2, split_eight, 0)
    even = b % 2 == 0
    odd = jnp.logical_not(even)
    pl.when(even & has_up)(pass_next)
    pl.when(odd & has_down)(pass_prev)
    pl.when(even & has_down)(pass_prev)
    pl.when(odd & has_up)(pass_next)
    arrived(4 + sib)
    arrived(4 + (sib + 2) % 4)
    turn_own()
    gather_main(0, False)
    gather_left(0, False)

    def took_prev():
        @pl.when(has_down)
        def _():
            arrived(sib)
            arrived((sib + 2) % 4)

        turn_prev()

    def took_next():
        @pl.when(has_up)
        def _():
            arrived(9 - core)

        @pl.when(has_up & (core == 1))
        def _():
            arrived(10, SHORT)

        turn_next()

    @pl.when(even)
    def _():
        took_next()
        took_prev()

    @pl.when(odd)
    def _():
        took_prev()
        took_next()

    gather_main(1, True)

    acc[...] = jnp.zeros(acc.shape, F32)
    side[...] = jnp.zeros(side.shape, F32)

    def multiply_main(q, _):
        both = jnp.dot(o_main[q], g_both[q, :, :256], preferred_element_type=F32)
        third = jnp.dot(o_main[q, :304], g_lo[q], preferred_element_type=F32)
        last = jnp.dot(o_left[q], g_last[q, :, :256], preferred_element_type=F32)
        acc[...] += both[:304] + both[304:] + third + last
        return 0

    def multiply_side(q, _):
        both = jnp.dot(o_main[q], g_both[q, :, 256:], preferred_element_type=F32)
        last = jnp.dot(o_left[q], g_last[q, :, 256:], preferred_element_type=F32)
        both = both[:304] + both[304:]
        side[...] += both[:, :128] + both[:, 128:] + last
        return 0

    lax.fori_loop(0, 2, multiply_main, 0)

    def packed(half):
        v = ufold[pl.ds(pl.multiple_of(STEP * half, 8), 160), :]
        row = jnp.zeros((40, 128), F32)
        for a in range(4):
            row = jnp.where(group_of_lane == a, v[40 * a : 40 * a + 40], row)
        return row

    def unpacked(v):
        parts = [v if a == 0 else pltpu.roll(v, 128 - 32 * a, 1) for a in range(4)]
        return jnp.concatenate(parts, axis=0)[:HALF]

    def send(i, source, target, device, recv=None):
        return pltpu.make_async_remote_copy(
            src_ref=source, dst_ref=target, send_sem=osend.at[i], recv_sem=orecv.at[i if recv is None else recv],
            device_id=device, device_id_type=MESH,
        )

    theirs = pl.ds(pl.multiple_of(STEP * (1 - core), 8), HALF)
    mine = pl.ds(pl.multiple_of(STEP * core, 8), HALF)
    swap = [send(0, acc.at[theirs], ra, sibling), send(1, lpack, ral, sibling)]
    swap[0].start()
    gather_left(1, True)
    swap[0].wait_recv()
    q0 = acc[mine, :128] + ra[:, :128]
    q1 = acc[mine, 128:256] + ra[:, 128:]
    q_ref[0], q_ref[1] = q0, q1
    cross = [send(2, q_ref.at[1 - chip], rq, beside), send(3, ql_ref, rql, beside)]
    cross[0].start()
    hi, lo = split(jnp.concatenate([q0, q1], axis=1))
    edges = jnp.dot(hi, hot_send[...], preferred_element_type=F32)
    edges = edges + jnp.dot(lo, hot_send[...], preferred_element_type=F32)
    for i in range(2):
        e = jnp.concatenate([edges[:, 128 * i : 128 * i + 128], jnp.zeros((8, 128), F32)], axis=0)
        for a in range(3):
            ht[i, 40 * a : 40 * a + 40] = e[40 * a : 40 * a + 40] + jnp.where(
                lane_id >= EDGE, pltpu.roll(e[120:160], 96 - 32 * a, 1), 0.0
            )
    heads = [send(4 + i, ht.at[0], hr.at[chip], peers[4 + i], 4 + chip) for i in range(2)]
    tails = send(6, ht.at[1], tr.at[chip], (up, core), 6 + chip)

    def with_up(name, *copies):
        for c in copies:
            pl.when(has_up)(c.start if name == "start" else c.wait_send)

    def with_down(name, *copies):
        for c in copies:
            pl.when(has_down)(c.start if name == "start" else c.wait_send)

    with_down("start", heads[1])
    with_up("start", tails)
    with_down("start", heads[0])
    lax.fori_loop(0, 2, multiply_side, 0)
    u = side[...]
    u = u + pltpu.roll(u, 64, 1)
    ufold[...] = u + pltpu.roll(u, 32, 1)
    lpack[...] = packed(1 - core)
    swap[1].start()
    own_left = packed(core)
    swap[1].wait_recv()
    ql_ref[...] = own_left + ral[...]
    head_ql = [send(9 + i, ql_ref, qh.at[chip], peers[4 + i], 9 + chip) for i in range(2)]
    tail_ql = send(11, ql_ref, qt.at[chip], (up, core), 11 + chip)
    with_down("start", head_ql[1])
    with_up("start", tail_ql)
    with_down("start", head_ql[0])
    cross[1].start()
    for c in cross:
        c.wait_recv()
    s = slot_of_column(iota((1, 128), 1) + 128 * chip)
    box1 = os1 + s
    keep = (box1 >= gs1) & (box1 < gs2) & (box1 < os2)
    own = jnp.where(keep, q_ref[chip] + rq[...], 0.0)
    box1 = os1 + slot_of_column(256 + (iota((1, 128), 1) & 31))
    keep = (box1 >= gs1) & (box1 < gs2) & (box1 < os2)
    own_left = unpacked(jnp.where(keep, ql_ref[...] + rql[...], 0.0))
    @pl.when(has_up)
    def _():
        for i in range(2):
            send(4 + i, ht.at[0], hr.at[i], peers[4], 4 + i).wait_recv()
            send(9, ql_ref, qh.at[i], peers[4], 9 + i).wait_recv()

    @pl.when(jnp.logical_not(has_up))
    def _():
        hr[...] = jnp.zeros(hr.shape, F32)
        qh[...] = jnp.zeros(qh.shape, F32)

    takes_tails = has_down & (chip == 0)

    @pl.when(takes_tails)
    def _():
        for i in range(2):
            send(6, ht.at[1], tr.at[i], peers[4], 6 + i).wait_recv()
            send(11, ql_ref, qt.at[i], peers[4], 11 + i).wait_recv()

    @pl.when(jnp.logical_not(takes_tails))
    def _():
        tr[...] = jnp.zeros(tr.shape, F32)
        qt[...] = jnp.zeros(qt.shape, F32)

    def edge_rows(v):
        thirds = [pltpu.roll(v[40 * a : 40 * a + 40], 32 * a + 32, 1) for a in range(3)]
        quarter = jnp.where(lane_id < 32, thirds[0], jnp.where(lane_id < 64, thirds[1], thirds[2]))
        return jnp.concatenate([v, quarter], axis=0)[:HALF]

    near = [edge_rows(v[0] + v[1]) for v in (hr, tr)]
    hi, lo = split(jnp.concatenate([*near, unpacked(qh[0] + qh[1]), unpacked(qt[0] + qt[1])], axis=1))
    moved = jnp.dot(hi, hot_recv[...], preferred_element_type=F32) + jnp.dot(
        lo, hot_recv[...], preferred_element_type=F32
    )
    v0, v1 = own + moved[:, :128], own_left + moved[:, 128:]
    v_ref[0], v_ref[1] = v0, v1
    last = send(8, v_ref, fr, sibling)
    last.start()
    for i, v in enumerate((v0, v1)):
        fin[i, mine] = v
    last.wait_recv()
    for i in range(2):
        fin[i, theirs] = fr[i]
        tt[i] = fin[i].T
    out[0:64] = tt[0, pl.ds(pl.multiple_of(64 * core, 8), 64), :F]
    out[64:72] = tt[1, pl.ds(pl.multiple_of(8 * o, 8), 8), :F]

    for c in (to_beside, to_sibling, hand_on(1, 4 + far), *swap, *cross, last):
        c.wait_send()
    with_up("wait_send", to_prev_segment(0), to_prev_segment(1), hand_on(4, 8 + core), tails, tail_ql)
    with_down("wait_send", hand_on(2, o), hand_on(3, far), *heads, *head_ql)

    @pl.when(has_up & (core == 0))
    def _():
        hand_on(5, 10, SHORT).wait_send()

    @pl.when(has_down & (o < 2))
    def _():
        for i in range(2):
            to_next_segment(i, TILES).wait_send()

    @pl.when(has_down & (o == 2))
    def _():
        for i in range(2):
            to_next_segment(i, SHORT).wait_send()


def body(density, operators, owner_count, group_count, target_slot, source_box):
    vmem = pl.BlockSpec(memory_space=pltpu.VMEM)
    scratch = [
        pltpu.VMEM((ROWS, F), F32),
        pltpu.VMEM(owner_count[None].shape, I32),
        pltpu.VMEM(group_count[None].shape, I32),
        pltpu.VMEM((1, OFFS, CAP), I32),
        pltpu.VMEM((1, OFFS, CAP), I32),
        pltpu.VMEM((12, TILES, 8, 128), F32),
        pltpu.VMEM((OFFS, 304, F), F32),
        pltpu.VMEM((2, 608, 2048), BF16),
        pltpu.VMEM((2, 304, 1024), BF16),
        pltpu.VMEM((3, 592, 256), BF16),
        pltpu.VMEM((4, 1024), I32),
        pltpu.VMEM((1, 512), I32),
        pltpu.VMEM((2, 2048, 512), BF16),
        pltpu.VMEM((2, 2048, 256), BF16),
        pltpu.VMEM((2, 1024, 384), BF16),
        pltpu.VMEM((304, 256), F32),
        pltpu.VMEM((304, 128), F32),
        pltpu.VMEM((304, 128), F32),
        pltpu.VMEM((256, 256), BF16),
        pltpu.VMEM((512, 256), BF16),
        pltpu.VMEM((40, 128), F32),
        pltpu.VMEM((HALF, 256), F32),
        pltpu.VMEM((40, 128), F32),
        pltpu.VMEM((2, HALF, 128), F32),
        pltpu.VMEM((40, 128), F32),
        pltpu.VMEM((2, 120, 128), F32),
        pltpu.VMEM((HALF, 128), F32),
        pltpu.VMEM((40, 128), F32),
        pltpu.VMEM((2, 120, 128), F32),
        pltpu.VMEM((2, 120, 128), F32),
        pltpu.VMEM((2, 40, 128), F32),
        pltpu.VMEM((2, 40, 128), F32),
        pltpu.VMEM((2, HALF, 128), F32),
        pltpu.VMEM((2, HALF, 128), F32),
        pltpu.VMEM((2, 384, 128), F32),
        pltpu.VMEM((2, 128, 384), F32),
        pltpu.SemaphoreType.DMA((5,)),
        pltpu.SemaphoreType.DMA((OFFS,)),
        pltpu.SemaphoreType.DMA((5,)),
        pltpu.SemaphoreType.DMA((6,)),
        pltpu.SemaphoreType.DMA((12,)),
        pltpu.SemaphoreType.DMA((12,)),
        pltpu.SemaphoreType.DMA((13,)),
    ]
    return pl.pallas_call(
        kernel,
        out_shape=jax.ShapeDtypeStruct((ROWS, F), F32),
        in_specs=[pl.BlockSpec(memory_space=pltpu.HBM)] * 6,
        out_specs=vmem,
        scratch_shapes=scratch,
        compiler_params=pltpu.CompilerParams(
            collective_id=0, has_side_effects=True, vmem_limit_bytes=60 * 2**20
        ),
        name="translate",
    )(density, operators, owner_count[None], group_count[None], target_slot, source_box)


def solution(mesh):
    placed = (P(("box", "op"), None), P("op", None, None), P(), P(), P("box", "op", None), P("box", "op", None))
    return jax.shard_map(
        body, mesh=mesh, in_specs=placed, out_specs=P(("box", "op"), None), check_vma=False
    )
```

```python
import jax
import jax.numpy as jnp
from jax import lax
from jax.experimental import pallas as pl
from jax.experimental.pallas import tpu as pltpu
from jax.sharding import PartitionSpec as P

MESH = pl.DeviceIdType.MESH
F32, BF16, I32 = jnp.float32, jnp.bfloat16, jnp.int32
ROWS = 72
CAP = 288
EDGE = 96
F = 296
HALF = 152
STEP = 144
OFFS = 16
TILES = 21
SHORT = 15


def iota(shape, dim):
    return lax.broadcasted_iota(I32, shape, dim)


def split(v):
    hi = v.astype(BF16)
    lo = (v - hi.astype(F32)).astype(BF16)
    return hi, lo


def slot_of_column(col):
    main = 72 * (col >> 6) + (col & 63)
    c = col & 31
    left = 72 * (c >> 3) + 64 + (c & 7)
    return jnp.where(col < 256, main, left)


def start_at(counts, index):
    lane = iota(counts.shape, 1)
    return jnp.sum(jnp.where(lane < index, counts.astype(F32), 0.0), axis=1, keepdims=True).astype(I32)


def kernel(
    den_hbm, ops, ocnt_hbm, gcnt_hbm, tgt_hbm, src_hbm, out,
    den, ocnt, gcnt, tgt, src, rx, stage, o_main, o_left, xt, pmain, pleft, g_both, g_lo, g_last, acc, side, ufold,
    hot_send, hot_recv, lpack, ra, ral, q_ref, ql_ref, ht, rq, rql, hr, tr, qh, qt, v_ref, fr, fin, tt,
    in_sem, op_sem, ici_send, sib_send, rsem, osend, orecv,
):
    b, o = lax.axis_index("box"), lax.axis_index("op")
    n = lax.axis_size("box")
    core, chip = o % 2, o // 2
    far, sib = (o + 2) % 4, o + 1 - 2 * core
    up, down = (b + 1) % n, (b + n - 1) % n
    sibling, beside = (b, sib), (b, far)
    peers = [sibling, beside, (up, o), (up, far), (down, o), (down, far)]
    has_down, has_up = b > 0, b < n - 1

    def op_copy(k):
        return pltpu.make_async_copy(ops.at[k], stage.at[k, pl.ds(0, F)], op_sem.at[k])

    barrier = pltpu.get_barrier_semaphore()


    def greet(some):
        for peer in some:
            pl.semaphore_signal(barrier, inc=1, device_id=peer, device_id_type=MESH)

    greet(peers[:2])
    pl.when(has_up)(lambda: greet(peers[2:4]))
    pl.when(has_down)(lambda: greet(peers[4:]))
    pairs = ((den_hbm, den), (ocnt_hbm, ocnt), (gcnt_hbm, gcnt), (tgt_hbm, tgt), (src_hbm, src))
    inputs = [pltpu.make_async_copy(a, v, in_sem.at[i]) for i, (a, v) in enumerate(pairs)]
    for c in inputs:
        c.start()
    inputs[0].wait()

    me = 4 + o
    for lt in range(3):
        parts = [den[8 * (lt + 3 * g) : 8 * (lt + 3 * g) + 8, 256:F] for g in range(3)]
        rx[me, lt] = jnp.concatenate([*parts, jnp.zeros((8, 8), F32)], axis=1)
    for rt in range(9):
        for h in range(2):
            rx[me, 3 + 2 * rt + h] = den[8 * rt : 8 * rt + 8, 128 * h : 128 * h + 128]

    def block_copy(here, there, count, send, device):
        return pltpu.make_async_remote_copy(
            src_ref=rx.at[here, pl.ds(0, count)], dst_ref=rx.at[there, pl.ds(0, count)],
            send_sem=send, recv_sem=rsem.at[there], device_id=device, device_id_type=MESH,
        )

    pl.semaphore_wait(barrier, jnp.where(has_up & has_down, 6, 4))

    def to_prev_segment(i):
        return block_copy(me, o, TILES, ici_send.at[1 + i], peers[2 + i])

    def to_next_segment(i, count):
        return block_copy(me, 8 + o, count, ici_send.at[3 + i], peers[4 + i])

    to_beside = block_copy(me, me, TILES, ici_send.at[0], beside)
    to_sibling = block_copy(me, me, TILES, sib_send.at[0], sibling)
    for i in (1, 0):

        @pl.when(has_up)
        def _():
            to_prev_segment(i).start()

        @pl.when(has_down & (o < 2))
        def _():
            to_next_segment(i, TILES).start()

        @pl.when(has_down & (o == 2))
        def _():
            to_next_segment(i, SHORT).start()

    to_beside.start()
    to_sibling.start()
    for k in range(OFFS):
        op_copy(k).start()

    for c in inputs[1:]:
        c.wait()
    counts_o, counts_g = ocnt[...], gcnt[...]
    os0, os1, os2 = (start_at(counts_o, b + i) for i in (-1, 0, 1))
    gs1, gs2 = (start_at(counts_g, b + i) for i in (0, 1))
    shift = gs1 - os1
    m = src[0]
    before, own = m - os0, m - os1
    before = 512 + jnp.where(before < 256, before, before - 256)
    own = jnp.where(own < 256, own, own + 192)
    place = jnp.where(m < os1, before, jnp.where(m < os2, own, 256 + m - os2))
    place = jnp.where(tgt[0] < CAP, place, -1)
    j = iota((CAP, 384), 0) + shift
    j = jnp.where(j < 0, j + CAP, jnp.where(j >= CAP, j - CAP, j))
    turn = jnp.where(j == slot_of_column(iota((CAP, 384), 1)), 1.0, 0.0).astype(F32)
    turned = jnp.dot(place.astype(F32), turn, precision=lax.Precision.HIGHEST, preferred_element_type=F32)
    turned = (turned + 0.25 * jnp.where(turned < 0, -1.0, 1.0)).astype(I32)
    lane_id = iota((1, 128), 1)
    group_of_lane = lane_id >> 5
    for i in range(4):
        pmain[i : i + 1] = jnp.concatenate([turned[k : k + 1, :256] for k in range(4 * i, 4 * i + 4)], axis=1)
        row = jnp.zeros((1, 128), I32)
        for a in range(4):
            row = jnp.where(group_of_lane == a, turned[4 * i + a : 4 * i + a + 1, 256:384], row)
        pleft[:, 128 * i : 128 * i + 128] = row

    s = slot_of_column(iota((256, 128), 0))
    lane = iota((256, 128), 1)
    is_head = (s >= CAP - EDGE) & (os1 + s - CAP >= gs1) & (s - (CAP - EDGE) == lane)
    box1 = os1 + s
    tail = jnp.where((box1 >= os2) & (box1 < gs2), box1 - os2, jnp.where(box1 + CAP < gs2, box1 + CAP - os2, -1))
    hot_send[:, :128] = jnp.where(is_head, 1.0, 0.0).astype(BF16)
    hot_send[:, 128:] = jnp.where(tail == lane, 1.0, 0.0).astype(BF16)
    r = iota((512, 128), 0)
    c = r & 127
    s = slot_of_column(256 + (c & 31))
    head = jnp.where((s >= CAP - EDGE) & (os2 + s - CAP >= gs2), os2 - os1 + s - CAP, -1)
    box0 = os0 + s
    tail = jnp.where((box0 >= os1) & (box0 < gs1), box0, jnp.where(box0 + CAP < gs1, box0 + CAP, -1))
    tail = jnp.where(tail >= 0, tail - os1, -1)
    far_slot = jnp.where(c < 32, jnp.where(r < 384, head, tail), -1)
    near_slot = jnp.where(c < EDGE, jnp.where(r < 128, os2 - os1 + c - EDGE, c), -1)
    slot = jnp.where(r < 256, near_slot, far_slot)
    lane = iota((512, 128), 1)
    hot_recv[:, :128] = jnp.where(slot == slot_of_column(lane + 128 * chip), 1.0, 0.0).astype(BF16)
    hot_recv[:, 128:] = jnp.where((lane < 32) & (slot == slot_of_column(lane + 256)), 1.0, 0.0).astype(BF16)


    stage[:, pl.ds(F, 8), :] = jnp.zeros((OFFS, 8, F), F32)

    def split_eight(q, _):
        for a in range(8):
            k = 8 * q + a
            op_copy(k).wait()
            v = stage[k]
            hi = v.astype(BF16)
            hi32 = hi.astype(F32)
            lo32 = v - hi32
            o_main[q, :304, 256 * a : 256 * a + 256] = hi[:, :256]
            o_main[q, 304:, 256 * a : 256 * a + 256] = lo32[:, :256].astype(BF16)
            last = jnp.concatenate([hi32[:, 256:], hi32[:, 256:], lo32[:, 256:], jnp.zeros((304, 8), F32)], axis=1)
            o_left[q, :, 128 * a : 128 * a + 128] = last.astype(BF16)
        return 0

    def arrived(there, count=TILES):
        block_copy(there, there, count, ici_send.at[0], sibling).wait_recv()

    def hand_on(i, there, count=TILES):
        return block_copy(there, there, count, sib_send.at[i], sibling)

    def pass_own():
        arrived(4 + far)
        hand_on(1, 4 + far).start()

    def pass_prev():
        for i, there in ((2, o), (3, far)):
            arrived(there)
            hand_on(i, there).start()

    def pass_next():
        arrived(8 + core)
        hand_on(4, 8 + core).start()

        @pl.when(core == 0)
        def _():
            arrived(10, SHORT)
            hand_on(5, 10, SHORT).start()

    def row_tiles(segment, tiles):
        return [(4 * segment + r // 9, r % 9) for r in tiles]

    def wide_left(idx, rt):
        left = rx[idx, rt % 3]
        return rx[idx, 3 + 2 * rt], rx[idx, 4 + 2 * rt], pltpu.roll(left, 128 - 40 * (rt // 3), 1) if rt >= 3 else left

    def turn_rows(t, half, parts):
        cols = [jnp.concatenate(list(p), axis=0).T for p in zip(*parts)]
        v = jnp.concatenate([cols[0], cols[1], cols[2][:40]], axis=0)
        hi32 = v.astype(BF16).astype(F32)
        lo32 = v - hi32
        xt[t, :, 128 * half : 128 * half + 128] = jnp.concatenate(
            [hi32[:256], lo32[:256], hi32[256:F], lo32[256:F]], axis=0
        ).astype(BF16)

    def turn_own():
        for half in range(2):
            turn_rows(0, half, [wide_left(*a) for a in row_tiles(1, range(16 * half, 16 * half + 16))])

    def turn_next():
        turn_rows(1, 0, [wide_left(*a) for a in row_tiles(2, range(16))])
        parts = [wide_left(*a) for a in row_tiles(2, range(16, 24)) + row_tiles(1, range(32, 36))]
        turn_rows(1, 1, parts + [(jnp.zeros((8, 128), F32),) * 3] * 4)

    def turn_prev():
        parts = [wide_left(*a) for a in row_tiles(0, range(16))]
        folded = [wide_left(*a) for a in row_tiles(0, range(32, 36))]
        long = os1 - os0 > 256
        for r in range(4):
            parts[r] = tuple(jnp.where(long, x, y) for x, y in zip(folded[r], parts[r]))
        turn_rows(2, 0, parts)
        turn_rows(2, 1, [wide_left(*a) for a in row_tiles(0, range(16, 32))])

    def gathered(row, t):
        rows = xt[0] if t == 0 else jnp.concatenate([xt[1], xt[2]], axis=1)
        hot = jnp.where(iota((rows.shape[1], row.shape[1]), 0) + 256 * t == row, 1.0, 0.0).astype(BF16)
        return jnp.dot(rows, hot, preferred_element_type=F32)

    def put(q, a, g, left, add):
        tail = jnp.concatenate([g[512:592], g[512:552], jnp.zeros((8, g.shape[1]), F32)], axis=0)
        rows, short = pl.ds(256 * a, 256), pl.ds(128 * a, 128)
        for ref, at, columns, v in (
            (g_both, rows, pl.ds(256, 128) if left else pl.ds(0, 256), g[:256]),
            (g_both, rows, pl.ds(384, 128), g[256:512]) if left else (g_lo, rows, pl.ds(0, 256), g[256:512]),
            (g_last, short, pl.ds(256, 128) if left else pl.ds(0, 256), tail),
        ):
            v = v.astype(BF16)
            ref[q, at, columns] = ref[q, at, columns] + v if add else v

    def gather_main(t, add):
        def gather_eight(q, _):
            for h in range(2):
                g = gathered(pmain[pl.ds(2 * q + h, 1), :], t)
                for a in range(4):
                    put(q, 4 * h + a, g[:, 256 * a : 256 * a + 256], False, add)
            return 0

        lax.fori_loop(0, 2, gather_eight, 0)

    def gather_left(t, add):
        g = gathered(pleft[...], t)
        for k in range(OFFS):
            part = g[:, 128 * (k // 4) : 128 * (k // 4) + 128]
            put(k // 8, k % 8, jnp.where(group_of_lane == k % 4, part, 0.0), True, add)

    @pl.when(jnp.logical_not(has_down))
    def _():
        rx[0:4] = jnp.zeros((4, TILES, 8, 128), F32)

    @pl.when(jnp.logical_not(has_up))
    def _():
        rx[8:11] = jnp.zeros((3, TILES, 8, 128), F32)

    lax.fori_loop(0, 1, split_eight, 0)
    pass_own()
    lax.fori_loop(1, 2, split_eight, 0)
    even = b % 2 == 0
    odd = jnp.logical_not(even)
    pl.when(even & has_up)(pass_next)
    pl.when(odd & has_down)(pass_prev)
    pl.when(even & has_down)(pass_prev)
    pl.when(odd & has_up)(pass_next)
    arrived(4 + sib)
    arrived(4 + (sib + 2) % 4)
    turn_own()
    gather_main(0, False)
    gather_left(0, False)

    def took_prev():
        @pl.when(has_down)
        def _():
            arrived(sib)
            arrived((sib + 2) % 4)

        turn_prev()

    def took_next():
        @pl.when(has_up)
        def _():
            arrived(9 - core)

        @pl.when(has_up & (core == 1))
        def _():
            arrived(10, SHORT)

        turn_next()

    @pl.when(even)
    def _():
        took_next()
        took_prev()

    @pl.when(odd)
    def _():
        took_prev()
        took_next()

    gather_main(1, True)

    acc[...] = jnp.zeros(acc.shape, F32)
    side[...] = jnp.zeros(side.shape, F32)

    def multiply_main(q, _):
        both = jnp.dot(o_main[q], g_both[q, :, :256], preferred_element_type=F32)
        third = jnp.dot(o_main[q, :304], g_lo[q], preferred_element_type=F32)
        last = jnp.dot(o_left[q], g_last[q, :, :256], preferred_element_type=F32)
        acc[...] += both[:304] + both[304:] + third + last
        return 0

    def multiply_side(q, _):
        both = jnp.dot(o_main[q], g_both[q, :, 256:], preferred_element_type=F32)
        last = jnp.dot(o_left[q], g_last[q, :, 256:], preferred_element_type=F32)
        both = both[:304] + both[304:]
        side[...] += both[:, :128] + both[:, 128:] + last
        return 0

    lax.fori_loop(0, 2, multiply_main, 0)

    def packed(half):
        v = ufold[pl.ds(pl.multiple_of(STEP * half, 8), 160), :]
        row = jnp.zeros((40, 128), F32)
        for a in range(4):
            row = jnp.where(group_of_lane == a, v[40 * a : 40 * a + 40], row)
        return row

    def unpacked(v):
        parts = [v if a == 0 else pltpu.roll(v, 128 - 32 * a, 1) for a in range(4)]
        return jnp.concatenate(parts, axis=0)[:HALF]

    def send(i, source, target, device, recv=None):
        return pltpu.make_async_remote_copy(
            src_ref=source, dst_ref=target, send_sem=osend.at[i], recv_sem=orecv.at[i if recv is None else recv],
            device_id=device, device_id_type=MESH,
        )

    theirs = pl.ds(pl.multiple_of(STEP * (1 - core), 8), HALF)
    mine = pl.ds(pl.multiple_of(STEP * core, 8), HALF)
    swap = [send(0, acc.at[theirs], ra, sibling), send(1, lpack, ral, sibling)]
    swap[0].start()
    gather_left(1, True)
    swap[0].wait_recv()
    q0 = acc[mine, :128] + ra[:, :128]
    q1 = acc[mine, 128:256] + ra[:, 128:]
    q_ref[0], q_ref[1] = q0, q1
    cross = [send(2, q_ref.at[1 - chip], rq, beside), send(3, ql_ref, rql, beside)]
    cross[0].start()
    hi, lo = split(jnp.concatenate([q0, q1], axis=1))
    edges = jnp.dot(hi, hot_send[...], preferred_element_type=F32)
    edges = edges + jnp.dot(lo, hot_send[...], preferred_element_type=F32)
    for i in range(2):
        e = jnp.concatenate([edges[:, 128 * i : 128 * i + 128], jnp.zeros((8, 128), F32)], axis=0)
        for a in range(3):
            ht[i, 40 * a : 40 * a + 40] = e[40 * a : 40 * a + 40] + jnp.where(
                lane_id >= EDGE, pltpu.roll(e[120:160], 96 - 32 * a, 1), 0.0
            )
    heads = [send(4 + i, ht.at[0], hr.at[chip], peers[4 + i], 4 + chip) for i in range(2)]
    tails = send(6, ht.at[1], tr.at[chip], (up, core), 6 + chip)

    def with_up(name, *copies):
        for c in copies:
            pl.when(has_up)(c.start if name == "start" else c.wait_send)

    def with_down(name, *copies):
        for c in copies:
            pl.when(has_down)(c.start if name == "start" else c.wait_send)

    with_down("start", heads[1])
    with_up("start", tails)
    with_down("start", heads[0])
    lax.fori_loop(0, 2, multiply_side, 0)
    u = side[...]
    u = u + pltpu.roll(u, 64, 1)
    ufold[...] = u + pltpu.roll(u, 32, 1)
    lpack[...] = packed(1 - core)
    swap[1].start()
    own_left = packed(core)
    swap[1].wait_recv()
    ql_ref[...] = own_left + ral[...]
    head_ql = [send(9 + i, ql_ref, qh.at[chip], peers[4 + i], 9 + chip) for i in range(2)]
    tail_ql = send(11, ql_ref, qt.at[chip], (up, core), 11 + chip)
    with_down("start", head_ql[1])
    with_up("start", tail_ql)
    with_down("start", head_ql[0])
    cross[1].start()
    for c in cross:
        c.wait_recv()
    s = slot_of_column(iota((1, 128), 1) + 128 * chip)
    box1 = os1 + s
    keep = (box1 >= gs1) & (box1 < gs2) & (box1 < os2)
    own = jnp.where(keep, q_ref[chip] + rq[...], 0.0)
    box1 = os1 + slot_of_column(256 + (iota((1, 128), 1) & 31))
    keep = (box1 >= gs1) & (box1 < gs2) & (box1 < os2)
    own_left = unpacked(jnp.where(keep, ql_ref[...] + rql[...], 0.0))
    @pl.when(has_up)
    def _():
        for i in range(2):
            send(4 + i, ht.at[0], hr.at[i], peers[4], 4 + i).wait_recv()
            send(9, ql_ref, qh.at[i], peers[4], 9 + i).wait_recv()

    @pl.when(jnp.logical_not(has_up))
    def _():
        hr[...] = jnp.zeros(hr.shape, F32)
        qh[...] = jnp.zeros(qh.shape, F32)

    takes_tails = has_down & (chip == 0)

    @pl.when(takes_tails)
    def _():
        for i in range(2):
            send(6, ht.at[1], tr.at[i], peers[4], 6 + i).wait_recv()
            send(11, ql_ref, qt.at[i], peers[4], 11 + i).wait_recv()

    @pl.when(jnp.logical_not(takes_tails))
    def _():
        tr[...] = jnp.zeros(tr.shape, F32)
        qt[...] = jnp.zeros(qt.shape, F32)

    def edge_rows(v):
        thirds = [pltpu.roll(v[40 * a : 40 * a + 40], 32 * a + 32, 1) for a in range(3)]
        quarter = jnp.where(lane_id < 32, thirds[0], jnp.where(lane_id < 64, thirds[1], thirds[2]))
        return jnp.concatenate([v, quarter], axis=0)[:HALF]

    near = [edge_rows(v[0] + v[1]) for v in (hr, tr)]
    hi, lo = split(jnp.concatenate([*near, unpacked(qh[0] + qh[1]), unpacked(qt[0] + qt[1])], axis=1))
    moved = jnp.dot(hi, hot_recv[...], preferred_element_type=F32) + jnp.dot(
        lo, hot_recv[...], preferred_element_type=F32
    )
    v0, v1 = own + moved[:, :128], own_left + moved[:, 128:]
    v_ref[0], v_ref[1] = v0, v1
    last = send(8, v_ref, fr, sibling)
    last.start()
    for i, v in enumerate((v0, v1)):
        fin[i, mine] = v
    last.wait_recv()
    for i in range(2):
        fin[i, theirs] = fr[i]
        tt[i] = fin[i].T
    out[0:64] = tt[0, pl.ds(pl.multiple_of(64 * core, 8), 64), :F]
    out[64:72] = tt[1, pl.ds(pl.multiple_of(8 * o, 8), 8), :F]

    for c in (to_beside, to_sibling, hand_on(1, 4 + far), *swap, *cross, last):
        c.wait_send()
    with_up("wait_send", to_prev_segment(0), to_prev_segment(1), hand_on(4, 8 + core), tails, tail_ql)
    with_down("wait_send", hand_on(2, o), hand_on(3, far), *heads, *head_ql)

    @pl.when(has_up & (core == 0))
    def _():
        hand_on(5, 10, SHORT).wait_send()

    @pl.when(has_down & (o < 2))
    def _():
        for i in range(2):
            to_next_segment(i, TILES).wait_send()

    @pl.when(has_down & (o == 2))
    def _():
        for i in range(2):
            to_next_segment(i, SHORT).wait_send()


def body(density, operators, owner_count, group_count, target_slot, source_box):
    vmem = pl.BlockSpec(memory_space=pltpu.VMEM)
    scratch = [
        pltpu.VMEM((ROWS, F), F32),
        pltpu.VMEM(owner_count[None].shape, I32),
        pltpu.VMEM(group_count[None].shape, I32),
        pltpu.VMEM((1, OFFS, CAP), I32),
        pltpu.VMEM((1, OFFS, CAP), I32),
        pltpu.VMEM((12, TILES, 8, 128), F32),
        pltpu.VMEM((OFFS, 304, F), F32),
        pltpu.VMEM((2, 608, 2048), BF16),
        pltpu.VMEM((2, 304, 1024), BF16),
        pltpu.VMEM((3, 592, 256), BF16),
        pltpu.VMEM((4, 1024), I32),
        pltpu.VMEM((1, 512), I32),
        pltpu.VMEM((2, 2048, 512), BF16),
        pltpu.VMEM((2, 2048, 256), BF16),
        pltpu.VMEM((2, 1024, 384), BF16),
        pltpu.VMEM((304, 256), F32),
        pltpu.VMEM((304, 128), F32),
        pltpu.VMEM((304, 128), F32),
        pltpu.VMEM((256, 256), BF16),
        pltpu.VMEM((512, 256), BF16),
        pltpu.VMEM((40, 128), F32),
        pltpu.VMEM((HALF, 256), F32),
        pltpu.VMEM((40, 128), F32),
        pltpu.VMEM((2, HALF, 128), F32),
        pltpu.VMEM((40, 128), F32),
        pltpu.VMEM((2, 120, 128), F32),
        pltpu.VMEM((HALF, 128), F32),
        pltpu.VMEM((40, 128), F32),
        pltpu.VMEM((2, 120, 128), F32),
        pltpu.VMEM((2, 120, 128), F32),
        pltpu.VMEM((2, 40, 128), F32),
        pltpu.VMEM((2, 40, 128), F32),
        pltpu.VMEM((2, HALF, 128), F32),
        pltpu.VMEM((2, HALF, 128), F32),
        pltpu.VMEM((2, 384, 128), F32),
        pltpu.VMEM((2, 128, 384), F32),
        pltpu.SemaphoreType.DMA((5,)),
        pltpu.SemaphoreType.DMA((OFFS,)),
        pltpu.SemaphoreType.DMA((5,)),
        pltpu.SemaphoreType.DMA((6,)),
        pltpu.SemaphoreType.DMA((12,)),
        pltpu.SemaphoreType.DMA((12,)),
        pltpu.SemaphoreType.DMA((13,)),
    ]
    return pl.pallas_call(
        kernel,
        out_shape=jax.ShapeDtypeStruct((ROWS, F), F32),
        in_specs=[pl.BlockSpec(memory_space=pltpu.HBM)] * 6,
        out_specs=vmem,
        scratch_shapes=scratch,
        compiler_params=pltpu.CompilerParams(
            collective_id=0, has_side_effects=True, vmem_limit_bytes=60 * 2**20
        ),
        name="translate",
    )(density, operators, owner_count[None], group_count[None], target_slot, source_box)


def solution(mesh):
    placed = (P(("box", "op"), None), P("op", None, None), P(), P(), P("box", "op", None), P("box", "op", None))
    return jax.shard_map(
        body, mesh=mesh, in_specs=placed, out_specs=P(("box", "op"), None), check_vma=False
    )
```
